32 devices in a mesh: row: 8 (over y, x, core), col: 4 (over z).
Axes of the slice: x: 2, y: 2, z: 4, core: 2. Of those that a mesh axis runs over, the one named last changes fastest.
Arguments:
- object_field: float32 [2, 4096, 2048], P(None, 'row', 'col'), may hold values from -6 to 6
- probe: bfloat16 [2, 4, 256, 256], replicated, may hold values from -3 to 3
- patterns: float32 [256, 256, 256], P(('row', 'col')), may hold values from 0.3 to 4
- offsets: int32 [2, 256], P(None, ('row', 'col')), may hold values from 0 to 3840, as said below
- counts: int32 [8, 4], P('row', 'col'), may hold values from 1 to 8, as said below
Outputs:
- object_grad: float32 [2, 4096, 2048], P(None, 'row', 'col')
- probe_grad: float32 [2, 4, 256, 256], replicated
The draws below stay inside these ranges and needn't reach their ends.
Inputs may be any that keep to these rules, and one draw needn't show every extreme that they name: `offsets`: the patch of a slot held by the device at (r, c) lies inside object rows r * 512 - 128 to (r + 1) * 512 + 128 and columns c * 512 - 128 to (c + 1) * 512 + 128, and inside the object. `counts`: some device has all 8 slots live.
All inputs are finite; a program needn't handle non-finite values.
Results may differ from the reference program's by a relative error of at most 0.005.
Values sent between devices are 32-bit elements; how exact they have to be, the bound alone decides.
A program may use at most 128 MiB of HBM per device.

```python
import math
import jax
import jax.numpy as jnp
from jax import lax

PAT = 256
MODES = 4
TILE = 512
POS_DEV = 8
HALO = 128
OY = 4096
OX = 2048
NPOS = 256
N_ROW = 8
N_COL = 4


def draw_counts(key, part):
    key = jax.random.fold_in(key, 11)
    first, second, third = jax.random.split(key, 3)
    total = N_ROW * N_COL
    upper = jax.random.randint(first, (total,), 1, POS_DEV + 1)
    values = jax.random.randint(second, (total,), 0, 1048576) % upper + 1
    chosen = jax.random.randint(third, (), 0, total)
    values = jnp.where(jnp.arange(total) == chosen, POS_DEV, values)
    return values.reshape(N_ROW, N_COL).astype(jnp.int32)


def corner_draw(key, tile_index, count):
    lower = jnp.where(tile_index == 0, 0, -HALO)
    upper = jnp.where(tile_index == count - 1, TILE - PAT, TILE - PAT + HALO)
    spread = jax.random.randint(key, (NPOS,), 0, 1048576) % (upper - lower + 1)
    return (lower, upper, lower + spread)


def draw_offsets(key, part):
    key = jax.random.fold_in(key, 23)
    keys = jax.random.split(key, 3)
    index = jnp.arange(NPOS)
    device = index // POS_DEV
    slot_number = index % POS_DEV
    row_index = device // N_COL
    col_index = device % N_COL
    low_row, high_row, local_row = corner_draw(keys[0], row_index, N_ROW)
    low_col, high_col, local_col = corner_draw(keys[1], col_index, N_COL)
    base = jax.random.randint(keys[2], (N_ROW * N_COL,), 0, POS_DEV)[device]
    picks = [(base + which) % POS_DEV for which in range(4)]
    local_row = jnp.where(slot_number == picks[0], low_row, local_row)
    local_row = jnp.where(slot_number == picks[1], high_row, local_row)
    local_col = jnp.where(slot_number == picks[2], low_col, local_col)
    local_col = jnp.where(slot_number == picks[3], high_col, local_col)
    rows_out = row_index * TILE + local_row
    cols_out = col_index * TILE + local_col
    return jnp.stack([rows_out, cols_out]).astype(jnp.int32)


def steps_of(key, dims, shards, least, largest):
    factor_of = 1.0
    for dim, parts in shards:
        heights = jax.random.uniform(jax.random.fold_in(jax.random.fold_in(key, 6), dim), (parts,), jnp.float32, least / len(shards), largest / len(shards))
        factor_of = factor_of * jnp.repeat(jnp.exp(heights), dims[dim] // parts).reshape((-1,) + (1,) * (len(dims) - 1 - dim))
    return factor_of


def centred(key, shape, width, most, cuts=(), kind=jnp.bfloat16):
    array = jax.random.normal(key, shape, jnp.float32) * width
    if len(cuts) > 0:
        array = steps_of(key, shape, cuts, -0.22, 0.18) * array
    return jnp.clip(array, min=-most, max=most).astype(kind)


def setup_inputs(seed: int = 0) -> dict:
    seeds = jax.random.split(jax.random.key(seed), 6)
    object_field = centred(seeds[0], (2, OY, OX), 1.0, 6.0, ((1, 8), (2, 4)), jnp.float32)
    probe = centred(seeds[1], (2, MODES, PAT, PAT), 0.5, 3.0)
    patterns = jnp.clip(jnp.exp(math.log(4.0) - 2.5902671 * jax.random.uniform(seeds[2], (NPOS, PAT, PAT), jnp.float32) ** steps_of(seeds[2], (NPOS, PAT, PAT), ((0, 32),), -0.2, 0.2)), 0.3, 4.0)
    offsets = draw_offsets(jax.random.fold_in(seeds[5], 71), 0)
    counts = draw_counts(jax.random.fold_in(seeds[5], 71), 0)
    return {"object_field": object_field, "probe": probe, "patterns": patterns, "offsets": offsets, "counts": counts}


def tables(length):
    index = jnp.arange(length, dtype=jnp.int32)
    product = index[:, None] * index[None, :] % length
    angle = product.astype(jnp.float32) * (2.0 * math.pi / length)
    factor = 1.0 / math.sqrt(length)
    return ((jnp.cos(angle) * factor).astype(jnp.bfloat16), (-jnp.sin(angle) * factor).astype(jnp.bfloat16))

def right_dot(matrix, table):
    return jnp.einsum('kab,bc->kac', matrix.astype(jnp.float32), table.astype(jnp.float32), precision=lax.Precision.HIGHEST)

def left_dot(table, matrix):
    return jnp.einsum('ab,kbc->kac', table.astype(jnp.float32), matrix.astype(jnp.float32), precision=lax.Precision.HIGHEST)

def right_mult(real_part, imag_part, table_re, table_im):
    return (right_dot(real_part, table_re) - right_dot(imag_part, table_im), right_dot(real_part, table_im) + right_dot(imag_part, table_re))

def left_mult(table_re, table_im, real_part, imag_part):
    return (left_dot(table_re, real_part) - left_dot(table_im, imag_part), left_dot(table_re, imag_part) + left_dot(table_im, real_part))

def position(patch_re, patch_im, measured, probe_re, probe_im, table_re, table_im):
    probe_fr = probe_re.astype(jnp.float32)
    probe_fi = probe_im.astype(jnp.float32)
    exit_re = (probe_fr * patch_re - probe_fi * patch_im).astype(jnp.bfloat16)
    exit_im = (probe_fr * patch_im + probe_fi * patch_re).astype(jnp.bfloat16)
    half_re, half_im = right_mult(exit_re, exit_im, table_re, table_im)
    field_re, field_im = left_mult(table_re, table_im, half_re.astype(jnp.bfloat16), half_im.astype(jnp.bfloat16))
    intensity = lax.optimization_barrier(jnp.sum(field_re * field_re + field_im * field_im, axis=0))
    amplitude = jnp.sqrt(jnp.maximum(intensity, 1.0))
    ratio = 1.0 - measured / amplitude
    resid_re = (field_re * ratio).astype(jnp.bfloat16)
    resid_im = (field_im * ratio).astype(jnp.bfloat16)
    conj_im = -table_im
    back_re, back_im = right_mult(resid_re, resid_im, table_re, conj_im)
    wave_re, wave_im = left_mult(table_re, conj_im, back_re.astype(jnp.bfloat16), back_im.astype(jnp.bfloat16))
    object_re = lax.optimization_barrier(jnp.sum(probe_fr * wave_re + probe_fi * wave_im, axis=0))
    object_im = lax.optimization_barrier(jnp.sum(probe_fr * wave_im - probe_fi * wave_re, axis=0))
    update_re = patch_re * wave_re + patch_im * wave_im
    update_im = patch_re * wave_im - patch_im * wave_re
    return (jnp.stack([object_re, object_im]), jnp.stack([update_re, update_im]))

def reference(object_field, probe, patterns, offsets, counts):
    table_re, table_im = tables(PAT)
    flat_counts = counts.reshape(-1)
    zero_index = jnp.int32(0)

    def visit(number, carried):
        totals, probe_total = carried
        device = number // POS_DEV
        alive = number % POS_DEV < flat_counts[device]

        def work(inner):
            grad_total, probe_sum_now = inner
            start_row = offsets[0, number].astype(jnp.int32)
            start_col = offsets[1, number].astype(jnp.int32)
            patch = lax.dynamic_slice(object_field, (zero_index, start_row, start_col), (2, PAT, PAT))
            object_term, probe_term = position(patch[0], patch[1], patterns[number], probe[0], probe[1], table_re, table_im)
            previous = lax.dynamic_slice(grad_total, (zero_index, start_row, start_col), (2, PAT, PAT))
            grad_total = lax.dynamic_update_slice(grad_total, previous + object_term, (zero_index, start_row, start_col))
            return (grad_total, probe_sum_now + probe_term)
        return lax.cond(alive, work, lambda inner: inner, (totals, probe_total))
    start = (jnp.zeros(object_field.shape, jnp.float32), jnp.zeros((2, MODES, PAT, PAT), jnp.float32))
    object_grad, probe_grad = lax.fori_loop(0, NPOS, visit, start)
    return (object_grad, probe_grad)
```

```python
import math

import jax
import jax.numpy as jnp
import ml_dtypes
import numpy as np
from jax import lax
from jax.experimental import pallas as pl
from jax.experimental.pallas import tpu as pltpu
from jax.sharding import PartitionSpec as P

F32 = jnp.float32
BF16 = jnp.bfloat16


def shifted(block, axis, distance):
    devices = range(lax.axis_size(axis))
    route = [(i - distance, i) for i in devices if i - distance in devices]
    return lax.ppermute(block, axis, route)


def tables(length):
    index = np.arange(length)
    product = index[:, None] * index[None, :] % length
    angle = product.astype(np.float32) * np.float32(2.0 * math.pi / length)
    factor = np.float32(1.0 / math.sqrt(length))
    re = (np.cos(angle) * factor).astype(ml_dtypes.bfloat16)
    im = (-np.sin(angle) * factor).astype(ml_dtypes.bfloat16)
    half = length // 2
    right = []
    left = []
    for parity in range(2):
        a, b = re[:half, parity::2], im[:half, parity::2]
        right.append(np.block([[a, b], [-b, a]]))
        a, b = re[parity::2, :half], im[parity::2, :half]
        left.append(np.block([[a, -b], [b, a]]))
    order = np.concatenate([index[0::2], index[1::2]])
    spread = (index[:, None] == order[None, :]).astype(ml_dtypes.bfloat16)
    return np.stack(right + left + [spread])


def mm(a, b):
    return jnp.dot(a, b, preferred_element_type=F32)


SUB = 8
LANES = 128


def rows_up(block, shift):
    tiles = block.reshape(-1, SUB, LANES)
    tiles = pltpu.roll(tiles, lax.rem(SUB - shift, SUB), 1)
    near = lax.broadcasted_iota(jnp.int32, (1, SUB, LANES), 1) < SUB - shift
    return jnp.where(near, tiles[:-1], tiles[1:]).reshape(-1, LANES)


def rows_down(block, shift):
    tiles = pltpu.roll(block.reshape(-1, SUB, LANES), lax.rem(shift, SUB), 1)
    near = lax.broadcasted_iota(jnp.int32, (1, SUB, LANES), 1) >= shift
    zero = jnp.zeros((1, SUB, LANES), F32)
    high = jnp.concatenate([tiles, zero], axis=0)
    low = jnp.concatenate([zero, tiles], axis=0)
    return jnp.where(near, high, low).reshape(-1, LANES)


def kernel(
    rows_ref, cols_ref, count_ref,
    object_ref, left_ref, right_ref, top_ref, bottom_ref, probe_ref, pattern_lo, pattern_hi, table_ref,
    up_ref, middle_ref, down_ref, update_ref,
    ext, totals, patch, field, residual, term, sems,
):
    number = pl.program_id(0)
    last = pl.num_programs(0) - 1
    tile_rows, tile_cols = object_ref.shape[1:]
    margin = top_ref.shape[1]
    modes, width = probe_ref.shape[1:3]
    half = width // 2
    lanes = LANES

    @pl.when(number == 0)
    def _():
        body = pl.ds(margin, tile_rows)
        copies = [
            pltpu.make_async_copy(object_ref, ext.at[:, body, pl.ds(margin, tile_cols)], sems.at[0]),
            pltpu.make_async_copy(left_ref, ext.at[:, body, pl.ds(0, margin)], sems.at[1]),
            pltpu.make_async_copy(
                right_ref, ext.at[:, body, pl.ds(margin + tile_cols, margin)], sems.at[2]
            ),
            pltpu.make_async_copy(top_ref, ext.at[:, pl.ds(0, margin), :], sems.at[3]),
            pltpu.make_async_copy(
                bottom_ref, ext.at[:, pl.ds(margin + tile_rows, margin), :], sems.at[4]
            ),
        ]
        for copy in copies:
            copy.start()
        totals[...] = jnp.zeros_like(totals)
        update_ref[...] = jnp.zeros_like(update_ref)
        for copy in copies:
            copy.wait()

    @pl.when(number < count_ref[0])
    def _():
        row = rows_ref[number]
        col = cols_ref[number]
        limit = ext.shape[2] - width - lanes
        base = pl.multiple_of(jnp.minimum(col // lanes * lanes, limit), lanes)
        shift = col - base
        tall = width + SUB
        row_base = pl.multiple_of(jnp.minimum(row // SUB * SUB, ext.shape[1] - tall), SUB)
        row_shift = row - row_base
        lane = lax.broadcasted_iota(jnp.int32, (width, lanes), 1)
        back = lax.rem(lanes - shift, lanes)
        ahead = lax.rem(shift, lanes)
        near = lane < lanes - shift
        for part in range(2):
            pieces = [
                pltpu.roll(
                    rows_up(
                        ext[part, pl.ds(row_base, tall), pl.ds(base + t * lanes, lanes)], row_shift
                    ),
                    back,
                    1,
                )
                for t in range(width // lanes + 1)
            ]
            for t in range(width // lanes):
                patch[part, :, t * lanes : (t + 1) * lanes] = jnp.where(
                    near, pieces[t], pieces[t + 1]
                )

        r_even, r_odd = table_ref[0], table_ref[1]
        l_even, l_odd = table_ref[2], table_ref[3]
        spread = table_ref[4]

        intensity = [jnp.zeros((half, width), F32) for _ in range(2)]
        for k in range(modes):
            o_re, o_im = patch[0], patch[1]
            p_re = probe_ref[0, k].astype(F32)
            p_im = probe_ref[1, k].astype(F32)
            x_re = p_re * o_re - p_im * o_im
            x_im = p_re * o_im + p_im * o_re
            s = jnp.concatenate(
                [x_re[:, :half] + x_re[:, half:], x_im[:, :half] + x_im[:, half:]], axis=1
            ).astype(BF16)
            d = jnp.concatenate(
                [x_re[:, :half] - x_re[:, half:], x_im[:, :half] - x_im[:, half:]], axis=1
            ).astype(BF16)
            y_even = mm(s, r_even)
            y_odd = mm(d, r_odd)
            for parity, table in enumerate((l_even, l_odd)):
                if parity == 0:
                    a = y_even[:half] + y_even[half:]
                    b = y_odd[:half] + y_odd[half:]
                else:
                    a = y_even[:half] - y_even[half:]
                    b = y_odd[:half] - y_odd[half:]
                u = jnp.concatenate(
                    [
                        jnp.concatenate([a[:, :half], b[:, :half]], axis=1),
                        jnp.concatenate([a[:, half:], b[:, half:]], axis=1),
                    ],
                    axis=0,
                ).astype(BF16)
                f = mm(table, u)
                field[k, parity] = f
                intensity[parity] += f[:half] * f[:half] + f[half:] * f[half:]

        for parity in range(2):
            rows_of = (0, pl.ds(parity, half, 2), slice(None))
            measured = jnp.concatenate([pattern_lo[rows_of], pattern_hi[rows_of]], axis=1)
            coarse = measured.astype(BF16)
            fine = (measured - coarse.astype(F32)).astype(BF16)
            measured = mm(coarse, spread) + mm(fine, spread)
            ratio = 1.0 - measured * lax.rsqrt(jnp.maximum(intensity[parity], 1.0))
            here = slice(parity * half, (parity + 1) * half)
            for k in range(modes):
                c_re = (field[k, parity, :half] * ratio).astype(BF16)
                c_im = (field[k, parity, half:] * ratio).astype(BF16)
                residual[k, 0, here, :half] = c_re[:, :half]
                residual[k, 0, here, half:] = c_im[:, :half]
                residual[k, 1, here, :half] = c_re[:, half:]
                residual[k, 1, here, half:] = c_im[:, half:]

        for k in range(modes):
            g_even = mm(residual[k, 0], l_even)
            g_odd = mm(residual[k, 1], l_odd)
            a = g_even + g_odd
            b = g_even - g_odd
            waves = []
            for parity, table in enumerate((r_even, r_odd)):
                here = slice(parity * half, (parity + 1) * half)
                v = jnp.concatenate(
                    [
                        jnp.concatenate([a[here, :half], b[here, :half]], axis=1),
                        jnp.concatenate([a[here, half:], b[here, half:]], axis=1),
                    ],
                    axis=0,
                ).astype(BF16)
                waves.append(mm(table, v))
            for part in range(2):
                wave = waves[0] + waves[1] if part == 0 else waves[0] - waves[1]
                w_re, w_im = wave[:half], wave[half:]
                here = slice(part * half, (part + 1) * half)
                p_re = probe_ref[0, k, here].astype(F32)
                p_im = probe_ref[1, k, here].astype(F32)
                o_re, o_im = patch[0, here], patch[1, here]
                t_re = p_re * w_re + p_im * w_im
                t_im = p_re * w_im - p_im * w_re
                if k == 0:
                    term[0, here] = t_re
                    term[1, here] = t_im
                else:
                    term[0, here] += t_re
                    term[1, here] += t_im
                update_ref[0, k, here] += o_re * w_re + o_im * w_im
                update_ref[1, k, here] += o_re * w_im - o_im * w_re

        far = lane >= shift
        for part in range(2):
            pieces = [
                pltpu.roll(term[part, :, t * lanes : (t + 1) * lanes], ahead, 1)
                for t in range(width // lanes)
            ]
            for t in range(width // lanes + 1):
                low = pieces[t - 1] if t > 0 else 0.0
                high = pieces[t] if t < width // lanes else 0.0
                where = (part, pl.ds(row_base, tall), pl.ds(base + t * lanes, lanes))
                totals[where] += rows_down(jnp.where(far, high, low), row_shift)

    @pl.when(number == last)
    def _():
        copies = [
            pltpu.make_async_copy(totals.at[:, pl.ds(0, margin), :], up_ref, sems.at[0]),
            pltpu.make_async_copy(totals.at[:, pl.ds(margin, tile_rows), :], middle_ref, sems.at[1]),
            pltpu.make_async_copy(
                totals.at[:, pl.ds(margin + tile_rows, margin), :], down_ref, sems.at[2]
            ),
        ]
        for copy in copies:
            copy.start()
        for copy in copies:
            copy.wait()


def gradients(rows, cols, count, object_field, left, right, top, bottom, probe, patterns, table):
    slots, width = patterns.shape[:2]
    modes = probe.shape[1]
    tile_rows, tile_cols = object_field.shape[1:]
    margin = width // 2
    full = (2, tile_rows + 2 * margin, tile_cols + 2 * margin)
    anywhere = pl.BlockSpec(memory_space=pl.ANY)

    def whole(shape):
        return pl.BlockSpec(shape, lambda n, *_: (0,) * len(shape))

    flops = slots * modes * 8 * 2 * width**3
    return pl.pallas_call(
        kernel,
        grid_spec=pltpu.PrefetchScalarGridSpec(
            num_scalar_prefetch=3,
            grid=(slots,),
            in_specs=[anywhere] * 5
            + [
                whole(probe.shape),
                pl.BlockSpec((1, width, width // 2), lambda n, *_: (n, 0, 0)),
                pl.BlockSpec((1, width, width // 2), lambda n, *_: (n, 0, 1)),
                whole(table.shape),
            ],
            out_specs=[anywhere] * 3 + [whole(probe.shape)],
            scratch_shapes=[
                pltpu.VMEM(full, F32),
                pltpu.VMEM(full, F32),
                pltpu.VMEM((2, width, width), F32),
                pltpu.VMEM((modes, 2, width, width), F32),
                pltpu.VMEM((modes, 2, width, width), BF16),
                pltpu.VMEM((2, width, width), F32),
                pltpu.SemaphoreType.DMA((5,)),
            ],
        ),
        out_shape=[
            jax.ShapeDtypeStruct((2, margin, full[2]), F32),
            jax.ShapeDtypeStruct((2, tile_rows, full[2]), F32),
            jax.ShapeDtypeStruct((2, margin, full[2]), F32),
            jax.ShapeDtypeStruct(probe.shape, F32),
        ],
        compiler_params=pltpu.CompilerParams(vmem_limit_bytes=56 * 2**20),
        cost_estimate=pl.CostEstimate(
            flops=flops, bytes_accessed=16 * 2**20, transcendentals=slots * width * width
        ),
    )(rows, cols, count, object_field, left, right, top, bottom, probe, patterns, patterns, table)


def on_device(object_field, probe, patterns, offsets, counts):
    tile_rows, tile_cols = object_field.shape[1:]
    width = patterns.shape[1]
    margin = width // 2
    base_row = lax.axis_index("row") * tile_rows - margin
    base_col = lax.axis_index("col") * tile_cols - margin
    table = jnp.asarray(tables(width))

    left = shifted(object_field[:, :, tile_cols - margin :], "col", 1)
    right = shifted(object_field[:, :, :margin], "col", -1)
    tail = slice(tile_rows - margin, None)
    head = slice(None, margin)
    lower = jnp.concatenate([left[:, tail], object_field[:, tail], right[:, tail]], axis=2)
    upper = jnp.concatenate([left[:, head], object_field[:, head], right[:, head]], axis=2)
    top = shifted(lower, "row", 1)
    bottom = shifted(upper, "row", -1)

    up, middle, down, update = gradients(
        offsets[0] - base_row, offsets[1] - base_col, counts.reshape(-1),
        object_field, left, right, top, bottom, probe, patterns, table,
    )
    probe_grad = lax.psum(update, ("row", "col"))
    from_above = shifted(down, "row", 1)
    from_below = shifted(up, "row", -1)
    middle = middle.at[:, head].add(from_above).at[:, tail].add(from_below)
    from_left = shifted(middle[:, :, tile_cols + margin :], "col", 1)
    from_right = shifted(middle[:, :, :margin], "col", -1)
    object_grad = middle[:, :, margin : margin + tile_cols]
    object_grad = object_grad.at[:, :, :margin].add(from_left)
    object_grad = object_grad.at[:, :, tile_cols - margin :].add(from_right)
    return (object_grad, probe_grad)


def solution(mesh):
    in_specs = (
        P(None, "row", "col"),
        P(),
        P(("row", "col"), None, None),
        P(None, ("row", "col")),
        P("row", "col"),
    )
    out_specs = (P(None, "row", "col"), P())
    return jax.shard_map(
        on_device, mesh=mesh, in_specs=in_specs, out_specs=out_specs, check_vma=False
    )
```

```python
import math

import jax
import jax.numpy as jnp
import ml_dtypes
import numpy as np
from jax import lax
from jax.experimental import pallas as pl
from jax.experimental.pallas import tpu as pltpu
from jax.sharding import PartitionSpec as P

F32 = jnp.float32
BF16 = jnp.bfloat16


def tables(length):
    index = np.arange(length)
    product = index[:, None] * index[None, :] % length
    angle = product.astype(np.float32) * np.float32(2.0 * math.pi / length)
    factor = np.float32(1.0 / math.sqrt(length))
    re = (np.cos(angle) * factor).astype(ml_dtypes.bfloat16)
    im = (-np.sin(angle) * factor).astype(ml_dtypes.bfloat16)
    half = length // 2
    right = []
    left = []
    for parity in range(2):
        a, b = re[:half, parity::2], im[:half, parity::2]
        right.append(np.block([[a, b], [-b, a]]))
        a, b = re[parity::2, :half], im[parity::2, :half]
        left.append(np.block([[a, -b], [b, a]]))
    order = np.concatenate([index[0::2], index[1::2]])
    spread = (index[:, None] == order[None, :]).astype(ml_dtypes.bfloat16)
    return np.stack(right + left + [spread])


def mm(a, b):
    return jnp.dot(a, b, preferred_element_type=F32)


SUB = 8
LANES = 128


def rows_up(block, shift):
    tiles = block.reshape(-1, SUB, LANES)
    tiles = pltpu.roll(tiles, lax.rem(SUB - shift, SUB), 1)
    near = lax.broadcasted_iota(jnp.int32, (1, SUB, LANES), 1) < SUB - shift
    return jnp.where(near, tiles[:-1], tiles[1:]).reshape(-1, LANES)


def rows_down(block, shift):
    tiles = pltpu.roll(block.reshape(-1, SUB, LANES), lax.rem(shift, SUB), 1)
    near = lax.broadcasted_iota(jnp.int32, (1, SUB, LANES), 1) >= shift
    zero = jnp.zeros((1, SUB, LANES), F32)
    high = jnp.concatenate([tiles, zero], axis=0)
    low = jnp.concatenate([zero, tiles], axis=0)
    return jnp.where(near, high, low).reshape(-1, LANES)


def kernel(
    rows_ref, cols_ref, count_ref,
    object_ref, left_ref, right_ref, top_ref, bottom_ref, probe_ref, pattern_lo, pattern_hi, table_ref,
    up_ref, middle_ref, down_ref, update_ref,
    ext, totals, patch, field, residual, term, sems,
):
    number = pl.program_id(0)
    last = pl.num_programs(0) - 1
    tile_rows, tile_cols = object_ref.shape[1:]
    margin = top_ref.shape[1]
    modes, width = probe_ref.shape[1:3]
    half = width // 2
    lanes = LANES

    @pl.when(number == 0)
    def _():
        body = pl.ds(margin, tile_rows)
        copies = [
            pltpu.make_async_copy(object_ref, ext.at[:, body, pl.ds(margin, tile_cols)], sems.at[0]),
            pltpu.make_async_copy(left_ref, ext.at[:, body, pl.ds(0, margin)], sems.at[1]),
            pltpu.make_async_copy(
                right_ref, ext.at[:, body, pl.ds(margin + tile_cols, margin)], sems.at[2]
            ),
            pltpu.make_async_copy(top_ref, ext.at[:, pl.ds(0, margin), :], sems.at[3]),
            pltpu.make_async_copy(
                bottom_ref, ext.at[:, pl.ds(margin + tile_rows, margin), :], sems.at[4]
            ),
        ]
        for copy in copies:
            copy.start()
        totals[...] = jnp.zeros_like(totals)
        update_ref[...] = jnp.zeros_like(update_ref)
        for copy in copies:
            copy.wait()

    @pl.when(number < count_ref[0])
    def _():
        row = rows_ref[number]
        col = cols_ref[number]
        limit = ext.shape[2] - width - lanes
        base = pl.multiple_of(jnp.minimum(col // lanes * lanes, limit), lanes)
        shift = col - base
        tall = width + SUB
        row_base = pl.multiple_of(jnp.minimum(row // SUB * SUB, ext.shape[1] - tall), SUB)
        row_shift = row - row_base
        lane = lax.broadcasted_iota(jnp.int32, (width, lanes), 1)
        back = lax.rem(lanes - shift, lanes)
        ahead = lax.rem(shift, lanes)
        near = lane < lanes - shift
        for part in range(2):
            pieces = [
                pltpu.roll(
                    rows_up(
                        ext[part, pl.ds(row_base, tall), pl.ds(base + t * lanes, lanes)], row_shift
                    ),
                    back,
                    1,
                )
                for t in range(width // lanes + 1)
            ]
            for t in range(width // lanes):
                patch[part, :, t * lanes : (t + 1) * lanes] = jnp.where(
                    near, pieces[t], pieces[t + 1]
                )

        r_even, r_odd = table_ref[0], table_ref[1]
        l_even, l_odd = table_ref[2], table_ref[3]
        spread = table_ref[4]

        intensity = [jnp.zeros((half, width), F32) for _ in range(2)]
        for k in range(modes):
            o_re, o_im = patch[0], patch[1]
            p_re = probe_ref[0, k].astype(F32)
            p_im = probe_ref[1, k].astype(F32)
            x_re = p_re * o_re - p_im * o_im
            x_im = p_re * o_im + p_im * o_re
            s = jnp.concatenate(
                [x_re[:, :half] + x_re[:, half:], x_im[:, :half] + x_im[:, half:]], axis=1
            ).astype(BF16)
            d = jnp.concatenate(
                [x_re[:, :half] - x_re[:, half:], x_im[:, :half] - x_im[:, half:]], axis=1
            ).astype(BF16)
            y_even = mm(s, r_even)
            y_odd = mm(d, r_odd)
            for parity, table in enumerate((l_even, l_odd)):
                if parity == 0:
                    a = y_even[:half] + y_even[half:]
                    b = y_odd[:half] + y_odd[half:]
                else:
                    a = y_even[:half] - y_even[half:]
                    b = y_odd[:half] - y_odd[half:]
                u = jnp.concatenate(
                    [
                        jnp.concatenate([a[:, :half], b[:, :half]], axis=1),
                        jnp.concatenate([a[:, half:], b[:, half:]], axis=1),
                    ],
                    axis=0,
                ).astype(BF16)
                f = mm(table, u)
                field[k, parity] = f
                intensity[parity] += f[:half] * f[:half] + f[half:] * f[half:]

        for parity in range(2):
            rows_of = (0, pl.ds(parity, half, 2), slice(None))
            measured = jnp.concatenate([pattern_lo[rows_of], pattern_hi[rows_of]], axis=1)
            coarse = measured.astype(BF16)
            fine = (measured - coarse.astype(F32)).astype(BF16)
            measured = mm(coarse, spread) + mm(fine, spread)
            ratio = 1.0 - measured * lax.rsqrt(jnp.maximum(intensity[parity], 1.0))
            here = slice(parity * half, (parity + 1) * half)
            for k in range(modes):
                c_re = (field[k, parity, :half] * ratio).astype(BF16)
                c_im = (field[k, parity, half:] * ratio).astype(BF16)
                residual[k, 0, here, :half] = c_re[:, :half]
                residual[k, 0, here, half:] = c_im[:, :half]
                residual[k, 1, here, :half] = c_re[:, half:]
                residual[k, 1, here, half:] = c_im[:, half:]

        for k in range(modes):
            g_even = mm(residual[k, 0], l_even)
            g_odd = mm(residual[k, 1], l_odd)
            a = g_even + g_odd
            b = g_even - g_odd
            waves = []
            for parity, table in enumerate((r_even, r_odd)):
                here = slice(parity * half, (parity + 1) * half)
                v = jnp.concatenate(
                    [
                        jnp.concatenate([a[here, :half], b[here, :half]], axis=1),
                        jnp.concatenate([a[here, half:], b[here, half:]], axis=1),
                    ],
                    axis=0,
                ).astype(BF16)
                waves.append(mm(table, v))
            for part in range(2):
                wave = waves[0] + waves[1] if part == 0 else waves[0] - waves[1]
                w_re, w_im = wave[:half], wave[half:]
                here = slice(part * half, (part + 1) * half)
                p_re = probe_ref[0, k, here].astype(F32)
                p_im = probe_ref[1, k, here].astype(F32)
                o_re, o_im = patch[0, here], patch[1, here]
                t_re = p_re * w_re + p_im * w_im
                t_im = p_re * w_im - p_im * w_re
                if k == 0:
                    term[0, here] = t_re
                    term[1, here] = t_im
                else:
                    term[0, here] += t_re
                    term[1, here] += t_im
                update_ref[0, k, here] += o_re * w_re + o_im * w_im
                update_ref[1, k, here] += o_re * w_im - o_im * w_re

        far = lane >= shift
        for part in range(2):
            pieces = [
                pltpu.roll(term[part, :, t * lanes : (t + 1) * lanes], ahead, 1)
                for t in range(width // lanes)
            ]
            for t in range(width // lanes + 1):
                low = pieces[t - 1] if t > 0 else 0.0
                high = pieces[t] if t < width // lanes else 0.0
                where = (part, pl.ds(row_base, tall), pl.ds(base + t * lanes, lanes))
                totals[where] += rows_down(jnp.where(far, high, low), row_shift)

    @pl.when(number == last)
    def _():
        copies = [
            pltpu.make_async_copy(totals.at[:, pl.ds(0, margin), :], up_ref, sems.at[0]),
            pltpu.make_async_copy(totals.at[:, pl.ds(margin, tile_rows), :], middle_ref, sems.at[1]),
            pltpu.make_async_copy(
                totals.at[:, pl.ds(margin + tile_rows, margin), :], down_ref, sems.at[2]
            ),
        ]
        for copy in copies:
            copy.start()
        for copy in copies:
            copy.wait()


def gradients(rows, cols, count, object_field, left, right, top, bottom, probe, patterns, table):
    slots, width = patterns.shape[:2]
    modes = probe.shape[1]
    tile_rows, tile_cols = object_field.shape[1:]
    margin = width // 2
    full = (2, tile_rows + 2 * margin, tile_cols + 2 * margin)
    anywhere = pl.BlockSpec(memory_space=pl.ANY)

    def whole(shape):
        return pl.BlockSpec(shape, lambda n, *_: (0,) * len(shape))

    flops = slots * modes * 8 * 2 * width**3
    return pl.pallas_call(
        kernel,
        grid_spec=pltpu.PrefetchScalarGridSpec(
            num_scalar_prefetch=3,
            grid=(slots,),
            in_specs=[anywhere] * 5
            + [
                whole(probe.shape),
                pl.BlockSpec((1, width, width // 2), lambda n, *_: (n, 0, 0)),
                pl.BlockSpec((1, width, width // 2), lambda n, *_: (n, 0, 1)),
                whole(table.shape),
            ],
            out_specs=[anywhere] * 3 + [whole(probe.shape)],
            scratch_shapes=[
                pltpu.VMEM(full, F32),
                pltpu.VMEM(full, F32),
                pltpu.VMEM((2, width, width), F32),
                pltpu.VMEM((modes, 2, width, width), F32),
                pltpu.VMEM((modes, 2, width, width), BF16),
                pltpu.VMEM((2, width, width), F32),
                pltpu.SemaphoreType.DMA((5,)),
            ],
        ),
        out_shape=[
            jax.ShapeDtypeStruct((2, margin, full[2]), F32),
            jax.ShapeDtypeStruct((2, tile_rows, full[2]), F32),
            jax.ShapeDtypeStruct((2, margin, full[2]), F32),
            jax.ShapeDtypeStruct(probe.shape, F32),
        ],
        compiler_params=pltpu.CompilerParams(vmem_limit_bytes=56 * 2**20),
        cost_estimate=pl.CostEstimate(
            flops=flops, bytes_accessed=16 * 2**20, transcendentals=slots * width * width
        ),
    )(rows, cols, count, object_field, left, right, top, bottom, probe, patterns, patterns, table)


class Move:
    def __init__(self, src, dst, sems, index, target, sends=None, lands=None):
        self.copy = pltpu.make_async_remote_copy(
            src_ref=src,
            dst_ref=dst,
            send_sem=sems[0].at[index],
            recv_sem=sems[1].at[index],
            device_id=target,
            device_id_type=pl.DeviceIdType.MESH,
        )
        self.sends = sends
        self.lands = lands

    def start(self):
        when(self.sends, self.copy.start)

    def arrive(self):
        when(self.lands, self.copy.wait_recv)

    def leave(self):
        when(self.sends, self.copy.wait_send)


def when(condition, action):
    if condition is None:
        action()
    else:
        pl.when(condition)(lambda: action())


class Place:
    def __init__(self):
        self.row, self.col = lax.axis_index("row"), lax.axis_index("col")
        self.rows, self.cols = lax.axis_size("row"), lax.axis_size("col")
        self.has_up, self.has_down = self.row > 0, self.row < self.rows - 1
        self.has_left, self.has_right = self.col > 0, self.col < self.cols - 1
        self.up, self.down = (self.row - 1, self.col), (self.row + 1, self.col)
        self.left, self.right = (self.row, self.col - 1), (self.row, self.col + 1)

    def greet(self, others=()):
        barrier = pltpu.get_barrier_semaphore()
        near = [
            (self.has_up, self.up),
            (self.has_down, self.down),
            (self.has_left, self.left),
            (self.has_right, self.right),
        ]

        def signal(target):
            pl.semaphore_signal(
                barrier, inc=1, device_id=target, device_id_type=pl.DeviceIdType.MESH
            )

        for condition, target in near:
            when(condition, lambda target=target: signal(target))
        for target in others:
            signal(target)
        peers = sum(condition.astype(jnp.int32) for condition, _ in near)
        pl.semaphore_wait(barrier, peers + len(others))


def halo_kernel(object_ref, left_ref, right_ref, top_ref, bottom_ref, send_sems, recv_sems):
    me = Place()
    tile_rows, tile_cols = object_ref.shape[1:]
    margin = top_ref.shape[1]
    sems = (send_sems, recv_sems)
    head, tail = pl.ds(0, margin), pl.ds(tile_rows - margin, margin)
    bands = [head, tail]
    if tile_rows > 2 * margin:
        bands.append(pl.ds(margin, tile_rows - 2 * margin))
    first, final = pl.ds(0, margin), pl.ds(tile_cols - margin, margin)
    centre = pl.ds(margin, tile_cols)
    beyond = pl.ds(margin + tile_cols, margin)
    me.greet()
    count = iter(range(send_sems.shape[0]))

    sides = []
    for band in bands:
        sides.append(
            (
                Move(object_ref.at[:, band, final], left_ref.at[:, band, :], sems, next(count),
                     me.right, me.has_right, me.has_left),
                Move(object_ref.at[:, band, first], right_ref.at[:, band, :], sems, next(count),
                     me.left, me.has_left, me.has_right),
            )
        )
    below = Move(object_ref.at[:, tail, :], top_ref.at[:, :, centre], sems, next(count),
                 me.down, me.has_down, me.has_up)
    above = Move(object_ref.at[:, head, :], bottom_ref.at[:, :, centre], sems, next(count),
                 me.up, me.has_up, me.has_down)
    moves = [move for pair in sides for move in pair] + [below, above]
    for move in moves:
        move.start()
    corners = []
    for number, (band, target, sends, lands, out_ref) in enumerate(
        [
            (head, me.up, me.has_up, me.has_down, bottom_ref),
            (tail, me.down, me.has_down, me.has_up, top_ref),
        ]
    ):
        for side, (src_ref, there, has) in enumerate(
            [(left_ref, first, me.has_left), (right_ref, beyond, me.has_right)]
        ):
            sides[number][side].arrive()
            move = Move(src_ref.at[:, band, :], out_ref.at[:, :, there], sems, next(count),
                        target, jnp.logical_and(sends, has), jnp.logical_and(lands, has))
            move.start()
            corners.append(move)
    for pair in sides[2:]:
        for move in pair:
            move.arrive()
    for move in [below, above] + corners:
        move.arrive()
    for move in moves + corners:
        move.leave()


def halo(object_field, margin):
    tile_rows, tile_cols = object_field.shape[1:]
    side = jax.ShapeDtypeStruct((2, tile_rows, margin), F32)
    edge = jax.ShapeDtypeStruct((2, margin, tile_cols + 2 * margin), F32)
    return pl.pallas_call(
        halo_kernel,
        in_specs=[pl.BlockSpec(memory_space=pl.ANY)],
        out_specs=[pl.BlockSpec(memory_space=pl.ANY)] * 4,
        out_shape=[side, side, edge, edge],
        scratch_shapes=[pltpu.SemaphoreType.DMA((12,)), pltpu.SemaphoreType.DMA((12,))],
        compiler_params=pltpu.CompilerParams(collective_id=0, has_side_effects=True),
    )(object_field)


def bits_of(count):
    return [1 << i for i in range(count.bit_length() - 1)]


def last_kernel(
    up_ref, middle_ref, down_ref, update_ref,
    object_ref, probe_ref,
    above, below, from_left, from_right, edges, total, landed,
    send_sems, recv_sems, sum_send, sum_recv, local_sems,
):
    me = Place()
    tile_rows, tile_cols = object_ref.shape[1:]
    margin = up_ref.shape[1]
    sems = (send_sems, recv_sems)
    head, tail = pl.ds(0, margin), pl.ds(tile_rows - margin, margin)
    first, beyond = pl.ds(0, margin), pl.ds(margin + tile_cols, margin)
    centre = pl.ds(margin, tile_cols)

    row_bits = [("row", bit) for bit in bits_of(me.rows)]
    col_bits = [("col", bit) for bit in bits_of(me.cols)]
    orders = [row_bits + col_bits, row_bits[:1] + row_bits[:0:-1] + col_bits]

    def partner(axis, bit):
        flip = lambda at: at + bit - 2 * bit * (at // bit % 2)
        return (flip(me.row), me.col) if axis == "row" else (me.row, flip(me.col))

    def half_of(axis, bit):
        return (me.row if axis == "row" else me.col) // bit % 2

    local = [
        pltpu.make_async_copy(update_ref, total, local_sems.at[0]),
        pltpu.make_async_copy(middle_ref.at[:, :, centre], object_ref, local_sems.at[1]),
    ]
    for side, cols in enumerate((first, beyond)):
        for end, band in enumerate((head, tail)):
            local.append(
                pltpu.make_async_copy(
                    middle_ref.at[:, band, cols],
                    edges.at[side, end],
                    local_sems.at[2 + 2 * side + end],
                )
            )
    for copy in local:
        copy.start()
    me.greet([partner(axis, bit) for axis, bit in orders[0] if bit > 1])

    count = iter(range(send_sems.shape[0]))
    corners = []
    for cols in (first, beyond):
        corners.append(
            (
                Move(down_ref.at[:, :, cols], above.at[:, :, cols], sems, next(count),
                     me.down, me.has_down, me.has_up),
                Move(up_ref.at[:, :, cols], below.at[:, :, cols], sems, next(count),
                     me.up, me.has_up, me.has_down),
            )
        )
    for pair in corners:
        for move in pair:
            move.start()

    size = update_ref.shape[0]
    bases = [[0], [0]]

    def halving(stream, step):
        lanes = pl.ds(stream * LANES, LANES)
        axis, bit = orders[stream][step]
        rows = size >> (step + 1)
        half = half_of(axis, bit)
        base = bases[stream][step]
        keep = pl.multiple_of(base + half * rows, SUB)
        give = pl.multiple_of(base + (1 - half) * rows, SUB)
        bases[stream].append(keep)
        source = update_ref if step == 0 else total
        return Move(
            source.at[pl.ds(give, rows), lanes],
            landed.at[pl.ds(size - 2 * rows, rows), lanes],
            (sum_send.at[stream], sum_recv.at[stream]), step, partner(axis, bit),
        )

    def add_half(stream, step, out_ref):
        lanes = pl.ds(stream * LANES, LANES)
        rows = size >> (step + 1)
        here = (pl.ds(bases[stream][step + 1], rows), lanes)
        out_ref[here] = total[here] + landed[pl.ds(size - 2 * rows, rows), lanes]

    def doubling(stream, step):
        lanes = pl.ds(stream * LANES, LANES)
        axis, bit = orders[stream][step]
        here = (pl.ds(bases[stream][step + 1], size >> (step + 1)), lanes)
        return Move(
            probe_ref.at[here], probe_ref.at[here],
            (sum_send.at[stream], sum_recv.at[stream]), steps + step, partner(axis, bit),
        )

    steps = len(orders[0])
    streams = range(2)
    sums = []
    current = [halving(stream, 0) for stream in streams]
    for move in current:
        move.start()

    flats = []
    if tile_rows > 2 * margin:
        inner = pl.ds(margin, tile_rows - 2 * margin)
        flats = [
            Move(middle_ref.at[:, inner, beyond], from_left.at[:, inner, :], sems, next(count),
                 me.right, me.has_right, me.has_left),
            Move(middle_ref.at[:, inner, first], from_right.at[:, inner, :], sems, next(count),
                 me.left, me.has_left, me.has_right),
        ]
    flats += [
        Move(down_ref.at[:, :, centre], above.at[:, :, centre], sems, next(count),
             me.down, me.has_down, me.has_up),
        Move(up_ref.at[:, :, centre], below.at[:, :, centre], sems, next(count),
             me.up, me.has_up, me.has_down),
    ]
    for move in flats:
        move.start()
    for copy in local:
        copy.wait()

    ends = []

    def send_ends():
        for side, (cols, out_ref, target, sends, lands) in enumerate(
            [
                (first, from_right, me.left, me.has_left, me.has_right),
                (beyond, from_left, me.right, me.has_right, me.has_left),
            ]
        ):
            for end, (band, got, has) in enumerate(
                [(head, above, me.has_up), (tail, below, me.has_down)]
            ):
                corners[side][end].arrive()

                def add(side=side, end=end, got=got, cols=cols):
                    edges[side, end] += got[:, :, cols]

                when(has, add)
                move = Move(edges.at[side, end], out_ref.at[:, band, :], sems, next(count),
                            target, sends, lands)
                move.start()
                ends.append(move)

    for step in range(steps):
        for stream in streams:
            move = current[stream]
            move.arrive()
            sums.append(move)
            add_half(stream, step, total if step < steps - 1 else probe_ref)
            if step < steps - 1:
                current[stream] = halving(stream, step + 1)
            else:
                current[stream] = doubling(stream, step)
            current[stream].start()
        if step == 0:
            send_ends()
    for step in range(steps - 1, -1, -1):
        for stream in streams:
            move = current[stream]
            move.arrive()
            sums.append(move)
            if step > 0:
                current[stream] = doubling(stream, step - 1)
                current[stream].start()

    for move in flats + ends:
        move.arrive()

    def from_above():
        object_ref[:, :margin, :] += above[:, :, margin : margin + tile_cols]

    def from_below():
        object_ref[:, tile_rows - margin :, :] += below[:, :, margin : margin + tile_cols]

    def add_left():
        object_ref[:, :, :margin] += from_left[...]

    def add_right():
        object_ref[:, :, tile_cols - margin :] += from_right[...]

    when(me.has_up, from_above)
    when(me.has_down, from_below)
    when(me.has_left, add_left)
    when(me.has_right, add_right)
    for move in [move for pair in corners for move in pair] + flats + ends + sums:
        move.leave()


def finish(up, middle, down, update):
    margin = up.shape[1]
    tile_rows = middle.shape[1]
    tile_cols = middle.shape[2] - 2 * margin
    width = update.shape[-1]
    flat = update.reshape(-1, width)
    steps = len(bits_of(lax.axis_size("row") * lax.axis_size("col")))
    vmem = pl.BlockSpec(memory_space=pltpu.VMEM)
    object_grad, probe_grad = pl.pallas_call(
        last_kernel,
        in_specs=[pl.BlockSpec(memory_space=pl.ANY)] * 4,
        out_specs=[vmem, vmem],
        out_shape=[
            jax.ShapeDtypeStruct((2, tile_rows, tile_cols), F32),
            jax.ShapeDtypeStruct(flat.shape, F32),
        ],
        scratch_shapes=[
            pltpu.VMEM(up.shape, F32),
            pltpu.VMEM(up.shape, F32),
            pltpu.VMEM((2, tile_rows, margin), F32),
            pltpu.VMEM((2, tile_rows, margin), F32),
            pltpu.VMEM((2, 2, 2, margin, margin), F32),
            pltpu.VMEM(flat.shape, F32),
            pltpu.VMEM(flat.shape, F32),
            pltpu.SemaphoreType.DMA((12,)),
            pltpu.SemaphoreType.DMA((12,)),
            pltpu.SemaphoreType.DMA((2, 2 * steps)),
            pltpu.SemaphoreType.DMA((2, 2 * steps)),
            pltpu.SemaphoreType.DMA((6,)),
        ],
        compiler_params=pltpu.CompilerParams(
            collective_id=1, has_side_effects=True, vmem_limit_bytes=40 * 2**20
        ),
    )(up, middle, down, flat)
    return object_grad, probe_grad.reshape(update.shape)


def on_device(object_field, probe, patterns, offsets, counts):
    tile_rows, tile_cols = object_field.shape[1:]
    width = patterns.shape[1]
    margin = width // 2
    base_row = lax.axis_index("row") * tile_rows - margin
    base_col = lax.axis_index("col") * tile_cols - margin
    table = jnp.asarray(tables(width))
    left, right, top, bottom = halo(object_field, margin)
    up, middle, down, update = gradients(
        offsets[0] - base_row, offsets[1] - base_col, counts.reshape(-1),
        object_field, left, right, top, bottom, probe, patterns, table,
    )
    return finish(up, middle, down, update)


def solution(mesh):
    in_specs = (
        P(None, "row", "col"),
        P(),
        P(("row", "col"), None, None),
        P(None, ("row", "col")),
        P("row", "col"),
    )
    out_specs = (P(None, "row", "col"), P())
    return jax.shard_map(
        on_device, mesh=mesh, in_specs=in_specs, out_specs=out_specs, check_vma=False
    )
```

```python
import math

import jax
import jax.numpy as jnp
import ml_dtypes
import numpy as np
from jax import lax
from jax.experimental import pallas as pl
from jax.experimental.pallas import tpu as pltpu
from jax.sharding import PartitionSpec as P

F32 = jnp.float32
BF16 = jnp.bfloat16


def tables(length):
    index = np.arange(length)
    product = index[:, None] * index[None, :] % length
    angle = product.astype(np.float32) * np.float32(2.0 * math.pi / length)
    factor = np.float32(1.0 / math.sqrt(length))
    re = (np.cos(angle) * factor).astype(ml_dtypes.bfloat16)
    im = (-np.sin(angle) * factor).astype(ml_dtypes.bfloat16)
    half = length // 2
    right = []
    left = []
    for parity in range(2):
        a, b = re[:half, parity::2], im[:half, parity::2]
        right.append(np.block([[a, b], [-b, a]]))
        a, b = re[parity::2, :half], im[parity::2, :half]
        left.append(np.block([[a, -b], [b, a]]))
    order = np.concatenate([index[0::2], index[1::2]])
    spread = (index[:, None] == order[None, :]).astype(ml_dtypes.bfloat16)
    return np.stack(right + left + [spread])


def mm(a, b):
    return jnp.dot(a, b, preferred_element_type=F32)


SUB = 8
LANES = 128


def rows_up(block, shift):
    tiles = block.reshape(-1, SUB, LANES)
    tiles = pltpu.roll(tiles, lax.rem(SUB - shift, SUB), 1)
    near = lax.broadcasted_iota(jnp.int32, (1, SUB, LANES), 1) < SUB - shift
    return jnp.where(near, tiles[:-1], tiles[1:]).reshape(-1, LANES)


def rows_down(block, shift):
    tiles = pltpu.roll(block.reshape(-1, SUB, LANES), lax.rem(shift, SUB), 1)
    near = lax.broadcasted_iota(jnp.int32, (1, SUB, LANES), 1) >= shift
    zero = jnp.zeros((1, SUB, LANES), F32)
    high = jnp.concatenate([tiles, zero], axis=0)
    low = jnp.concatenate([zero, tiles], axis=0)
    return jnp.where(near, high, low).reshape(-1, LANES)


def kernel(
    offsets_ref, count_ref,
    extended_ref, probe_hbm, patterns_ref, table_hbm,
    up_ref, middle_ref, down_ref, update_out,
    window, pattern, probe_ref, table_ref, totals, update_ref, patch, mixed, field, residual,
    measured_ref, term, sems,
):
    margin, tile_rows = up_ref.shape[1], middle_ref.shape[1]
    modes, width = probe_ref.shape[1:3]
    tile_cols = middle_ref.shape[2] - 2 * margin
    half = width // 2
    lanes = LANES
    tall, wide = window.shape[2:]
    chunk = 16
    live = count_ref[0, 0]
    first_row = lax.axis_index("row") * tile_rows - margin
    first_col = lax.axis_index("col") * tile_cols - margin

    def corner(number):
        row = offsets_ref[0, number] - first_row
        col = offsets_ref[1, number] - first_col
        row_base = jnp.minimum(row // SUB * SUB, totals.shape[1] - tall)
        col_base = jnp.minimum(col // lanes * lanes, totals.shape[2] - wide)
        return (
            pl.multiple_of(row_base, SUB), row - row_base,
            pl.multiple_of(col_base, lanes), col - col_base,
        )

    def fetches(number):
        slot = lax.rem(number, 2)
        row_base, _, col_base, _ = corner(number)
        return [
            pltpu.make_async_copy(
                extended_ref.at[:, pl.ds(row_base, tall), pl.ds(col_base, wide)],
                window.at[slot], sems.at[slot, 0],
            )
        ] + [
            pltpu.make_async_copy(
                patterns_ref.at[number, :, pl.ds(side * half, half)],
                pattern.at[slot, side], sems.at[slot, 1 + side],
            )
            for side in range(2)
        ]

    constants = [
        pltpu.make_async_copy(table_hbm, table_ref, sems.at[2, 0]),
        pltpu.make_async_copy(probe_hbm, probe_ref, sems.at[2, 1]),
    ]
    for copy in fetches(0) + constants:
        copy.start()
    totals[...] = jnp.zeros_like(totals)
    update_ref[...] = jnp.zeros_like(update_ref)
    for copy in constants:
        copy.wait()

    def visit(number, carried):
        slot = lax.rem(number, 2)
        row_base, row_shift, base, shift = corner(number)

        @pl.when(number + 1 < live)
        def _():
            for copy in fetches(number + 1):
                copy.start()

        for copy in fetches(number):
            copy.wait()

        lane = lax.broadcasted_iota(jnp.int32, (width, lanes), 1)
        back = lax.rem(lanes - shift, lanes)
        ahead = lax.rem(shift, lanes)
        near = lane < lanes - shift
        for part in range(2):
            pieces = [
                pltpu.roll(
                    rows_up(window[slot, part, :, t * lanes : (t + 1) * lanes], row_shift), back, 1
                )
                for t in range(width // lanes + 1)
            ]
            for t in range(width // lanes):
                patch[part, :, t * lanes : (t + 1) * lanes] = jnp.where(
                    near, pieces[t], pieces[t + 1]
                )

        r_even, r_odd = table_ref[0], table_ref[1]
        l_even, l_odd = table_ref[2], table_ref[3]
        spread = table_ref[4]

        for parity in range(2):
            rows_of = pl.ds(parity, half, 2)
            measured = jnp.concatenate(
                [pattern[slot, 0, rows_of, :], pattern[slot, 1, rows_of, :]], axis=1
            )
            coarse = measured.astype(BF16)
            fine = (measured - coarse.astype(F32)).astype(BF16)
            measured_ref[parity] = mm(coarse, spread) + mm(fine, spread)

        for k in range(modes):
            for start in range(0, width, chunk):
                here = slice(start, start + chunk)
                o_re, o_im = patch[0, here], patch[1, here]
                p_re = probe_ref[0, k, here].astype(F32)
                p_im = probe_ref[1, k, here].astype(F32)
                x_re = p_re * o_re - p_im * o_im
                x_im = p_re * o_im + p_im * o_re
                mixed[k, 0, here, :half] = (x_re[:, :half] + x_re[:, half:]).astype(BF16)
                mixed[k, 0, here, half:] = (x_im[:, :half] + x_im[:, half:]).astype(BF16)
                mixed[k, 1, here, :half] = (x_re[:, :half] - x_re[:, half:]).astype(BF16)
                mixed[k, 1, here, half:] = (x_im[:, :half] - x_im[:, half:]).astype(BF16)
            y_even = mm(mixed[k, 0], r_even)
            y_odd = mm(mixed[k, 1], r_odd)
            for parity, table in enumerate((l_even, l_odd)):
                if parity == 0:
                    a = y_even[:half] + y_even[half:]
                    b = y_odd[:half] + y_odd[half:]
                else:
                    a = y_even[:half] - y_even[half:]
                    b = y_odd[:half] - y_odd[half:]
                u = jnp.concatenate(
                    [
                        jnp.concatenate([a[:, :half], b[:, :half]], axis=1),
                        jnp.concatenate([a[:, half:], b[:, half:]], axis=1),
                    ],
                    axis=0,
                ).astype(BF16)
                field[k, parity] = mm(table, u)

        for parity in range(2):
            for start in range(0, half, chunk):
                top = slice(start, start + chunk)
                low = slice(half + start, half + start + chunk)
                here = slice(parity * half + start, parity * half + start + chunk)
                waves = [(field[k, parity, top], field[k, parity, low]) for k in range(modes)]
                intensity = sum(re * re + im * im for re, im in waves)
                ratio = 1.0 - measured_ref[parity, top] * lax.rsqrt(jnp.maximum(intensity, 1.0))
                for k, (re, im) in enumerate(waves):
                    c_re = (re * ratio).astype(BF16)
                    c_im = (im * ratio).astype(BF16)
                    residual[k, 0, here, :half] = c_re[:, :half]
                    residual[k, 0, here, half:] = c_im[:, :half]
                    residual[k, 1, here, :half] = c_re[:, half:]
                    residual[k, 1, here, half:] = c_im[:, half:]

        for k in range(modes):
            g_even = mm(residual[k, 0], l_even)
            g_odd = mm(residual[k, 1], l_odd)
            a = g_even + g_odd
            b = g_even - g_odd
            waves = []
            for parity, table in enumerate((r_even, r_odd)):
                here = slice(parity * half, (parity + 1) * half)
                v = jnp.concatenate(
                    [
                        jnp.concatenate([a[here, :half], b[here, :half]], axis=1),
                        jnp.concatenate([a[here, half:], b[here, half:]], axis=1),
                    ],
                    axis=0,
                ).astype(BF16)
                waves.append(mm(table, v))
            field[k, 0] = waves[0] + waves[1]
            field[k, 1] = waves[0] - waves[1]

        for part in range(2):
            for start in range(0, half, chunk):
                top = slice(start, start + chunk)
                low = slice(half + start, half + start + chunk)
                here = slice(part * half + start, part * half + start + chunk)
                o_re, o_im = patch[0, here], patch[1, here]
                t_re = t_im = 0.0
                for k in range(modes):
                    w_re, w_im = field[k, part, top], field[k, part, low]
                    p_re = probe_ref[0, k, here].astype(F32)
                    p_im = probe_ref[1, k, here].astype(F32)
                    t_re += p_re * w_re + p_im * w_im
                    t_im += p_re * w_im - p_im * w_re
                    update_ref[0, k, here] += o_re * w_re + o_im * w_im
                    update_ref[1, k, here] += o_re * w_im - o_im * w_re
                term[0, here] = t_re
                term[1, here] = t_im

        far = lane >= shift
        for part in range(2):
            pieces = [
                pltpu.roll(term[part, :, t * lanes : (t + 1) * lanes], ahead, 1)
                for t in range(width // lanes)
            ]
            for t in range(width // lanes + 1):
                low = pieces[t - 1] if t > 0 else 0.0
                high = pieces[t] if t < width // lanes else 0.0
                where = (part, pl.ds(row_base, tall), pl.ds(base + t * lanes, lanes))
                totals[where] += rows_down(jnp.where(far, high, low), row_shift)
        return carried

    lax.fori_loop(0, live, visit, 0)
    copies = [
        pltpu.make_async_copy(totals.at[:, pl.ds(0, margin), :], up_ref, sems.at[0, 0]),
        pltpu.make_async_copy(
            totals.at[:, pl.ds(margin + tile_rows, margin), :], down_ref, sems.at[0, 1]
        ),
        pltpu.make_async_copy(update_ref, update_out, sems.at[0, 2]),
    ] + [
        pltpu.make_async_copy(
            totals.at[part, pl.ds(margin, tile_rows), :], middle_ref.at[part], sems.at[1, part]
        )
        for part in range(2)
    ]
    for copy in copies:
        copy.start()
    for copy in copies:
        copy.wait()


def gradients(offsets, counts, extended, probe, patterns, table):
    slots, width = patterns.shape[:2]
    modes = probe.shape[1]
    margin = width // 2
    full = extended.shape
    tile_rows = full[1] - 2 * margin
    anywhere = pl.BlockSpec(memory_space=pl.ANY)
    scalars = pl.BlockSpec(memory_space=pltpu.SMEM)
    flops = slots * modes * 8 * 2 * width**3
    return pl.pallas_call(
        kernel,
        in_specs=[scalars] * 2 + [anywhere] * 4,
        out_specs=[anywhere] * 4,
        scratch_shapes=[
            pltpu.VMEM((2, 2, width + SUB, width + LANES), F32),
            pltpu.VMEM((2, 2, width, width // 2), F32),
            pltpu.VMEM(probe.shape, BF16),
            pltpu.VMEM(table.shape, BF16),
            pltpu.VMEM(full, F32),
            pltpu.VMEM(probe.shape, F32),
            pltpu.VMEM((2, width, width), F32),
            pltpu.VMEM((modes, 2, width, width), BF16),
            pltpu.VMEM((modes, 2, width, width), F32),
            pltpu.VMEM((modes, 2, width, width), BF16),
            pltpu.VMEM((2, width // 2, width), F32),
            pltpu.VMEM((2, width, width), F32),
            pltpu.SemaphoreType.DMA((3, 3)),
        ],
        out_shape=[
            jax.ShapeDtypeStruct((2, margin, full[2]), F32),
            jax.ShapeDtypeStruct((2, tile_rows, full[2]), F32),
            jax.ShapeDtypeStruct((2, margin, full[2]), F32),
            jax.ShapeDtypeStruct(probe.shape, F32),
        ],
        compiler_params=pltpu.CompilerParams(vmem_limit_bytes=60 * 2**20),
        cost_estimate=pl.CostEstimate(
            flops=flops, bytes_accessed=16 * 2**20, transcendentals=slots * width * width
        ),
    )(offsets, counts, extended, probe, patterns, table)


class Move:
    def __init__(self, src, dst, sems, index, target, sends=None, lands=None):
        self.copy = pltpu.make_async_remote_copy(
            src_ref=src,
            dst_ref=dst,
            send_sem=sems[0].at[index],
            recv_sem=sems[1].at[index],
            device_id=target,
            device_id_type=pl.DeviceIdType.MESH,
        )
        self.sends = sends
        self.lands = lands

    def start(self):
        when(self.sends, self.copy.start)

    def arrive(self):
        when(self.lands, self.copy.wait_recv)

    def leave(self):
        when(self.sends, self.copy.wait_send)


def when(condition, action):
    if condition is None:
        action()
    else:
        pl.when(condition)(lambda: action())


class Place:
    def __init__(self):
        self.row, self.col = lax.axis_index("row"), lax.axis_index("col")
        self.rows, self.cols = lax.axis_size("row"), lax.axis_size("col")
        self.has_up, self.has_down = self.row > 0, self.row < self.rows - 1
        self.has_left, self.has_right = self.col > 0, self.col < self.cols - 1
        self.up, self.down = (self.row - 1, self.col), (self.row + 1, self.col)
        self.left, self.right = (self.row, self.col - 1), (self.row, self.col + 1)

    def greet(self, others=()):
        barrier = pltpu.get_barrier_semaphore()
        near = [
            (self.has_up, self.up),
            (self.has_down, self.down),
            (self.has_left, self.left),
            (self.has_right, self.right),
        ]

        def signal(target):
            pl.semaphore_signal(
                barrier, inc=1, device_id=target, device_id_type=pl.DeviceIdType.MESH
            )

        for condition, target in near:
            when(condition, lambda target=target: signal(target))
        for target in others:
            signal(target)
        peers = sum(condition.astype(jnp.int32) for condition, _ in near)
        pl.semaphore_wait(barrier, peers + len(others))


def halo_kernel(object_ref, out_ref, send_sems, recv_sems, local_sem):
    me = Place()
    tile_rows, tile_cols = object_ref.shape[1:]
    margin = (out_ref.shape[1] - tile_rows) // 2
    sems = (send_sems, recv_sems)
    body, centre = pl.ds(margin, tile_rows), pl.ds(margin, tile_cols)
    own = pltpu.make_async_copy(object_ref, out_ref.at[:, body, centre], local_sem)
    bands = [(0, margin), (tile_rows - margin, margin)]
    if tile_rows > 2 * margin:
        bands.append((margin, tile_rows - 2 * margin))
    first, final = pl.ds(0, margin), pl.ds(tile_cols - margin, margin)
    beyond = pl.ds(margin + tile_cols, margin)
    above, below = pl.ds(0, margin), pl.ds(margin + tile_rows, margin)
    me.greet()
    count = iter(range(send_sems.shape[0]))

    sides = []
    for start, rows in bands:
        band, there = pl.ds(start, rows), pl.ds(margin + start, rows)
        sides.append(
            (
                Move(object_ref.at[:, band, final], out_ref.at[:, there, first], sems,
                     next(count), me.right, me.has_right, me.has_left),
                Move(object_ref.at[:, band, first], out_ref.at[:, there, beyond], sems,
                     next(count), me.left, me.has_left, me.has_right),
            )
        )
    strips = [
        Move(object_ref.at[:, pl.ds(tile_rows - margin, margin), :], out_ref.at[:, above, centre],
             sems, next(count), me.down, me.has_down, me.has_up),
        Move(object_ref.at[:, pl.ds(0, margin), :], out_ref.at[:, below, centre],
             sems, next(count), me.up, me.has_up, me.has_down),
    ]
    moves = [move for pair in sides for move in pair] + strips
    for move in moves:
        move.start()
    own.start()
    corners = []
    for number, (band, target, sends, lands, rows) in enumerate(
        [
            (pl.ds(margin, margin), me.up, me.has_up, me.has_down, below),
            (pl.ds(tile_rows, margin), me.down, me.has_down, me.has_up, above),
        ]
    ):
        for side, (cols, has) in enumerate([(first, me.has_left), (beyond, me.has_right)]):
            sides[number][side].arrive()
            move = Move(out_ref.at[:, band, cols], out_ref.at[:, rows, cols], sems, next(count),
                        target, jnp.logical_and(sends, has), jnp.logical_and(lands, has))
            move.start()
            corners.append(move)
    for pair in sides[2:]:
        for move in pair:
            move.arrive()
    for move in strips + corners:
        move.arrive()
    for move in moves + corners:
        move.leave()
    own.wait()


def halo(object_field, margin):
    tile_rows, tile_cols = object_field.shape[1:]
    anywhere = pl.BlockSpec(memory_space=pl.ANY)
    return pl.pallas_call(
        halo_kernel,
        in_specs=[anywhere],
        out_specs=anywhere,
        out_shape=jax.ShapeDtypeStruct((2, tile_rows + 2 * margin, tile_cols + 2 * margin), F32),
        scratch_shapes=[
            pltpu.SemaphoreType.DMA((12,)),
            pltpu.SemaphoreType.DMA((12,)),
            pltpu.SemaphoreType.DMA,
        ],
        compiler_params=pltpu.CompilerParams(
            collective_id=0, has_side_effects=True, vmem_limit_bytes=60 * 2**20
        ),
    )(object_field)


def bits_of(count):
    return [1 << i for i in range(count.bit_length() - 1)]


def last_kernel(
    up_ref, middle_ref, down_ref, update_ref,
    object_ref, probe_ref,
    above, below, from_left, from_right, edges, total, landed,
    send_sems, recv_sems, sum_send, sum_recv, local_sems,
):
    me = Place()
    tile_rows, tile_cols = object_ref.shape[1:]
    margin = up_ref.shape[1]
    sems = (send_sems, recv_sems)
    head, tail = pl.ds(0, margin), pl.ds(tile_rows - margin, margin)
    first, beyond = pl.ds(0, margin), pl.ds(margin + tile_cols, margin)
    centre = pl.ds(margin, tile_cols)

    row_bits = [("row", bit) for bit in bits_of(me.rows)]
    col_bits = [("col", bit) for bit in bits_of(me.cols)]
    orders = [row_bits + col_bits, row_bits[:1] + row_bits[:0:-1] + col_bits]

    def partner(axis, bit):
        flip = lambda at: at + bit - 2 * bit * (at // bit % 2)
        return (flip(me.row), me.col) if axis == "row" else (me.row, flip(me.col))

    def half_of(axis, bit):
        return (me.row if axis == "row" else me.col) // bit % 2

    local = [
        pltpu.make_async_copy(update_ref, total, local_sems.at[0]),
        pltpu.make_async_copy(middle_ref.at[:, :, centre], object_ref, local_sems.at[1]),
    ]
    for side, cols in enumerate((first, beyond)):
        for end, band in enumerate((head, tail)):
            local.append(
                pltpu.make_async_copy(
                    middle_ref.at[:, band, cols],
                    edges.at[side, end],
                    local_sems.at[2 + 2 * side + end],
                )
            )
    for copy in local:
        copy.start()
    me.greet([partner(axis, bit) for axis, bit in orders[0] if bit > 1])

    count = iter(range(send_sems.shape[0]))
    corners = []
    for cols in (first, beyond):
        corners.append(
            (
                Move(down_ref.at[:, :, cols], above.at[:, :, cols], sems, next(count),
                     me.down, me.has_down, me.has_up),
                Move(up_ref.at[:, :, cols], below.at[:, :, cols], sems, next(count),
                     me.up, me.has_up, me.has_down),
            )
        )

    size = update_ref.shape[0]
    bases = [[0], [0]]

    def halving(stream, step):
        lanes = pl.ds(stream * LANES, LANES)
        axis, bit = orders[stream][step]
        rows = size >> (step + 1)
        half = half_of(axis, bit)
        base = bases[stream][step]
        keep = pl.multiple_of(base + half * rows, SUB)
        give = pl.multiple_of(base + (1 - half) * rows, SUB)
        bases[stream].append(keep)
        source = update_ref if step == 0 else total
        return Move(
            source.at[pl.ds(give, rows), lanes],
            landed.at[pl.ds(size - 2 * rows, rows), lanes],
            (sum_send.at[stream], sum_recv.at[stream]), step, partner(axis, bit),
        )

    def add_half(stream, step, out_ref):
        lanes = pl.ds(stream * LANES, LANES)
        rows = size >> (step + 1)
        here = (pl.ds(bases[stream][step + 1], rows), lanes)
        out_ref[here] = total[here] + landed[pl.ds(size - 2 * rows, rows), lanes]

    def doubling(stream, step):
        lanes = pl.ds(stream * LANES, LANES)
        axis, bit = orders[stream][step]
        here = (pl.ds(bases[stream][step + 1], size >> (step + 1)), lanes)
        return Move(
            probe_ref.at[here], probe_ref.at[here],
            (sum_send.at[stream], sum_recv.at[stream]), steps + step, partner(axis, bit),
        )

    steps = len(orders[0])
    streams = range(2)
    sums = []
    current = [halving(stream, 0) for stream in streams]
    for move in current:
        move.start()
    for pair in corners:
        for move in pair:
            move.start()

    flats = []
    if tile_rows > 2 * margin:
        inner = pl.ds(margin, tile_rows - 2 * margin)
        flats = [
            Move(middle_ref.at[:, inner, beyond], from_left.at[:, inner, :], sems, next(count),
                 me.right, me.has_right, me.has_left),
            Move(middle_ref.at[:, inner, first], from_right.at[:, inner, :], sems, next(count),
                 me.left, me.has_left, me.has_right),
        ]
    for move in flats:
        move.start()
    for copy in local:
        copy.wait()

    ends = []

    def send_ends():
        for side, (cols, out_ref, target, sends, lands) in enumerate(
            [
                (first, from_right, me.left, me.has_left, me.has_right),
                (beyond, from_left, me.right, me.has_right, me.has_left),
            ]
        ):
            for end, (band, got, has) in enumerate(
                [(head, above, me.has_up), (tail, below, me.has_down)]
            ):
                corners[side][end].arrive()

                def add(side=side, end=end, got=got, cols=cols):
                    edges[side, end] += got[:, :, cols]

                when(has, add)
                move = Move(edges.at[side, end], out_ref.at[:, band, :], sems, next(count),
                            target, sends, lands)
                move.start()
                ends.append(move)

    for step in range(steps):
        for stream in streams:
            move = current[stream]
            move.arrive()
            sums.append(move)
            add_half(stream, step, total if step < steps - 1 else probe_ref)
            if step < steps - 1:
                current[stream] = halving(stream, step + 1)
            else:
                current[stream] = doubling(stream, step)
            current[stream].start()
        if step == 0:
            send_ends()
        if step == len(row_bits) - 1:
            strips = [
                Move(down_ref.at[:, :, centre], above.at[:, :, centre], sems, next(count),
                     me.down, me.has_down, me.has_up),
                Move(up_ref.at[:, :, centre], below.at[:, :, centre], sems, next(count),
                     me.up, me.has_up, me.has_down),
            ]
            for move in strips:
                move.start()
            flats += strips
    for step in range(steps - 1, -1, -1):
        for stream in streams:
            move = current[stream]
            move.arrive()
            sums.append(move)
            if step > 0:
                current[stream] = doubling(stream, step - 1)
                current[stream].start()

    for move in flats + ends:
        move.arrive()

    def from_above():
        object_ref[:, :margin, :] += above[:, :, margin : margin + tile_cols]

    def from_below():
        object_ref[:, tile_rows - margin :, :] += below[:, :, margin : margin + tile_cols]

    def add_left():
        object_ref[:, :, :margin] += from_left[...]

    def add_right():
        object_ref[:, :, tile_cols - margin :] += from_right[...]

    when(me.has_up, from_above)
    when(me.has_down, from_below)
    when(me.has_left, add_left)
    when(me.has_right, add_right)
    for move in [move for pair in corners for move in pair] + flats + ends + sums:
        move.leave()


def finish(up, middle, down, update):
    margin = up.shape[1]
    tile_rows = middle.shape[1]
    tile_cols = middle.shape[2] - 2 * margin
    width = update.shape[-1]
    flat = update.reshape(-1, width)
    steps = len(bits_of(lax.axis_size("row") * lax.axis_size("col")))
    vmem = pl.BlockSpec(memory_space=pltpu.VMEM)
    object_grad, probe_grad = pl.pallas_call(
        last_kernel,
        in_specs=[pl.BlockSpec(memory_space=pl.ANY)] * 4,
        out_specs=[vmem, vmem],
        out_shape=[
            jax.ShapeDtypeStruct((2, tile_rows, tile_cols), F32),
            jax.ShapeDtypeStruct(flat.shape, F32),
        ],
        scratch_shapes=[
            pltpu.VMEM(up.shape, F32),
            pltpu.VMEM(up.shape, F32),
            pltpu.VMEM((2, tile_rows, margin), F32),
            pltpu.VMEM((2, tile_rows, margin), F32),
            pltpu.VMEM((2, 2, 2, margin, margin), F32),
            pltpu.VMEM(flat.shape, F32),
            pltpu.VMEM(flat.shape, F32),
            pltpu.SemaphoreType.DMA((12,)),
            pltpu.SemaphoreType.DMA((12,)),
            pltpu.SemaphoreType.DMA((2, 2 * steps)),
            pltpu.SemaphoreType.DMA((2, 2 * steps)),
            pltpu.SemaphoreType.DMA((6,)),
        ],
        compiler_params=pltpu.CompilerParams(
            collective_id=1, has_side_effects=True, vmem_limit_bytes=60 * 2**20
        ),
    )(up, middle, down, flat)
    return object_grad, probe_grad.reshape(update.shape)


def on_device(object_field, probe, patterns, offsets, counts):
    width = patterns.shape[1]
    table = jnp.asarray(tables(width))
    extended = halo(object_field, width // 2)
    up, middle, down, update = gradients(offsets, counts, extended, probe, patterns, table)
    return finish(up, middle, down, update)


def solution(mesh):
    in_specs = (
        P(None, "row", "col"),
        P(),
        P(("row", "col"), None, None),
        P(None, ("row", "col")),
        P("row", "col"),
    )
    out_specs = (P(None, "row", "col"), P())
    return jax.shard_map(
        on_device, mesh=mesh, in_specs=in_specs, out_specs=out_specs, check_vma=False
    )
```

```python
import math

import jax
import jax.numpy as jnp
import ml_dtypes
import numpy as np
from jax import lax
from jax.experimental import pallas as pl
from jax.experimental.pallas import tpu as pltpu
from jax.sharding import PartitionSpec as P

F32 = jnp.float32
BF16 = jnp.bfloat16


def tables(length):
    index = np.arange(length)
    product = index[:, None] * index[None, :] % length
    angle = product.astype(np.float32) * np.float32(2.0 * math.pi / length)
    factor = np.float32(1.0 / math.sqrt(length))
    re = (np.cos(angle) * factor).astype(ml_dtypes.bfloat16)
    im = (-np.sin(angle) * factor).astype(ml_dtypes.bfloat16)
    half = length // 2
    right = []
    left = []
    for parity in range(2):
        a, b = re[:half, parity::2], im[:half, parity::2]
        right.append(np.block([[a, b], [-b, a]]))
        a, b = re[parity::2, :half], im[parity::2, :half]
        left.append(np.block([[a, -b], [b, a]]))
    order = np.concatenate([index[0::2], index[1::2]])
    spread = (index[:, None] == order[None, :]).astype(ml_dtypes.bfloat16)
    return np.stack(right + left + [spread])


def mm(a, b):
    return jnp.dot(a, b, preferred_element_type=F32)


SUB = 8
LANES = 128


def rows_up(block, shift):
    tiles = block.reshape(-1, SUB, LANES)
    tiles = pltpu.roll(tiles, lax.rem(SUB - shift, SUB), 1)
    near = lax.broadcasted_iota(jnp.int32, (1, SUB, LANES), 1) < SUB - shift
    return jnp.where(near, tiles[:-1], tiles[1:]).reshape(-1, LANES)


def rows_down(block, shift):
    tiles = pltpu.roll(block.reshape(-1, SUB, LANES), lax.rem(shift, SUB), 1)
    near = lax.broadcasted_iota(jnp.int32, (1, SUB, LANES), 1) >= shift
    zero = jnp.zeros((1, SUB, LANES), F32)
    high = jnp.concatenate([tiles, zero], axis=0)
    low = jnp.concatenate([zero, tiles], axis=0)
    return jnp.where(near, high, low).reshape(-1, LANES)


def kernel(
    offsets_ref, count_ref,
    extended_ref, probe_hbm, patterns_ref, table_hbm,
    up_ref, middle_ref, down_ref, update_out,
    window, pattern, probe_ref, table_ref, totals, update_ref, patch, mixed, field, residual,
    measured_ref, term, sems,
):
    margin, tile_rows = up_ref.shape[1], middle_ref.shape[1]
    modes, width = probe_ref.shape[1:3]
    tile_cols = middle_ref.shape[2] - 2 * margin
    half = width // 2
    lanes = LANES
    tall, wide = window.shape[2:]
    chunk = 16
    live = count_ref[0, 0]
    first_row = lax.axis_index("row") * tile_rows - margin
    first_col = lax.axis_index("col") * tile_cols - margin

    def corner(number):
        row = offsets_ref[0, number] - first_row
        col = offsets_ref[1, number] - first_col
        row_base = jnp.minimum(row // SUB * SUB, totals.shape[1] - tall)
        col_base = jnp.minimum(col // lanes * lanes, totals.shape[2] - wide)
        return (
            pl.multiple_of(row_base, SUB), row - row_base,
            pl.multiple_of(col_base, lanes), col - col_base,
        )

    def fetches(number):
        slot = lax.rem(number, 2)
        row_base, _, col_base, _ = corner(number)
        return [
            pltpu.make_async_copy(
                extended_ref.at[:, pl.ds(row_base, tall), pl.ds(col_base, wide)],
                window.at[slot], sems.at[slot, 0],
            )
        ] + [
            pltpu.make_async_copy(
                patterns_ref.at[number, :, pl.ds(side * half, half)],
                pattern.at[slot, side], sems.at[slot, 1 + side],
            )
            for side in range(2)
        ]

    constants = [
        pltpu.make_async_copy(table_hbm, table_ref, sems.at[2, 0]),
        pltpu.make_async_copy(probe_hbm, probe_ref, sems.at[2, 1]),
    ]
    for copy in fetches(0) + constants:
        copy.start()
    totals[...] = jnp.zeros_like(totals)
    update_ref[...] = jnp.zeros_like(update_ref)
    for copy in constants:
        copy.wait()

    def visit(number, carried):
        slot = lax.rem(number, 2)
        row_base, row_shift, base, shift = corner(number)

        @pl.when(number + 1 < live)
        def _():
            for copy in fetches(number + 1):
                copy.start()

        for copy in fetches(number):
            copy.wait()

        lane = lax.broadcasted_iota(jnp.int32, (width, lanes), 1)
        back = lax.rem(lanes - shift, lanes)
        ahead = lax.rem(shift, lanes)
        near = lane < lanes - shift
        for part in range(2):
            pieces = [
                pltpu.roll(
                    rows_up(window[slot, part, :, t * lanes : (t + 1) * lanes], row_shift), back, 1
                )
                for t in range(width // lanes + 1)
            ]
            for t in range(width // lanes):
                patch[part, :, t * lanes : (t + 1) * lanes] = jnp.where(
                    near, pieces[t], pieces[t + 1]
                )

        r_even, r_odd = table_ref[0], table_ref[1]
        l_even, l_odd = table_ref[2], table_ref[3]
        spread = table_ref[4]

        for parity in range(2):
            rows_of = pl.ds(parity, half, 2)
            measured = jnp.concatenate(
                [pattern[slot, 0, rows_of, :], pattern[slot, 1, rows_of, :]], axis=1
            )
            coarse = measured.astype(BF16)
            fine = (measured - coarse.astype(F32)).astype(BF16)
            measured_ref[parity] = mm(coarse, spread) + mm(fine, spread)

        for k in range(modes):
            for start in range(0, width, chunk):
                here = slice(start, start + chunk)
                o_re, o_im = patch[0, here], patch[1, here]
                p_re = probe_ref[0, k, here].astype(F32)
                p_im = probe_ref[1, k, here].astype(F32)
                x_re = p_re * o_re - p_im * o_im
                x_im = p_re * o_im + p_im * o_re
                mixed[k, 0, here, :half] = (x_re[:, :half] + x_re[:, half:]).astype(BF16)
                mixed[k, 0, here, half:] = (x_im[:, :half] + x_im[:, half:]).astype(BF16)
                mixed[k, 1, here, :half] = (x_re[:, :half] - x_re[:, half:]).astype(BF16)
                mixed[k, 1, here, half:] = (x_im[:, :half] - x_im[:, half:]).astype(BF16)
            y_even = mm(mixed[k, 0], r_even)
            y_odd = mm(mixed[k, 1], r_odd)
            for parity, table in enumerate((l_even, l_odd)):
                if parity == 0:
                    a = y_even[:half] + y_even[half:]
                    b = y_odd[:half] + y_odd[half:]
                else:
                    a = y_even[:half] - y_even[half:]
                    b = y_odd[:half] - y_odd[half:]
                u = jnp.concatenate(
                    [
                        jnp.concatenate([a[:, :half], b[:, :half]], axis=1),
                        jnp.concatenate([a[:, half:], b[:, half:]], axis=1),
                    ],
                    axis=0,
                ).astype(BF16)
                field[k, parity] = mm(table, u)

        for parity in range(2):
            for start in range(0, half, chunk):
                top = slice(start, start + chunk)
                low = slice(half + start, half + start + chunk)
                here = slice(parity * half + start, parity * half + start + chunk)
                waves = [(field[k, parity, top], field[k, parity, low]) for k in range(modes)]
                intensity = sum(re * re + im * im for re, im in waves)
                ratio = 1.0 - measured_ref[parity, top] * lax.rsqrt(jnp.maximum(intensity, 1.0))
                for k, (re, im) in enumerate(waves):
                    c_re = (re * ratio).astype(BF16)
                    c_im = (im * ratio).astype(BF16)
                    residual[k, 0, here, :half] = c_re[:, :half]
                    residual[k, 0, here, half:] = c_im[:, :half]
                    residual[k, 1, here, :half] = c_re[:, half:]
                    residual[k, 1, here, half:] = c_im[:, half:]

        for k in range(modes):
            g_even = mm(residual[k, 0], l_even)
            g_odd = mm(residual[k, 1], l_odd)
            a = g_even + g_odd
            b = g_even - g_odd
            waves = []
            for parity, table in enumerate((r_even, r_odd)):
                here = slice(parity * half, (parity + 1) * half)
                v = jnp.concatenate(
                    [
                        jnp.concatenate([a[here, :half], b[here, :half]], axis=1),
                        jnp.concatenate([a[here, half:], b[here, half:]], axis=1),
                    ],
                    axis=0,
                ).astype(BF16)
                waves.append(mm(table, v))
            field[k, 0] = waves[0] + waves[1]
            field[k, 1] = waves[0] - waves[1]

        for part in range(2):
            for start in range(0, half, chunk):
                top = slice(start, start + chunk)
                low = slice(half + start, half + start + chunk)
                here = slice(part * half + start, part * half + start + chunk)
                o_re, o_im = patch[0, here], patch[1, here]
                t_re = t_im = 0.0
                for k in range(modes):
                    w_re, w_im = field[k, part, top], field[k, part, low]
                    p_re = probe_ref[0, k, here].astype(F32)
                    p_im = probe_ref[1, k, here].astype(F32)
                    t_re += p_re * w_re + p_im * w_im
                    t_im += p_re * w_im - p_im * w_re
                    update_ref[0, k, here] += o_re * w_re + o_im * w_im
                    update_ref[1, k, here] += o_re * w_im - o_im * w_re
                term[0, here] = t_re
                term[1, here] = t_im

        far = lane >= shift
        for part in range(2):
            pieces = [
                pltpu.roll(term[part, :, t * lanes : (t + 1) * lanes], ahead, 1)
                for t in range(width // lanes)
            ]
            for t in range(width // lanes + 1):
                low = pieces[t - 1] if t > 0 else 0.0
                high = pieces[t] if t < width // lanes else 0.0
                where = (part, pl.ds(row_base, tall), pl.ds(base + t * lanes, lanes))
                totals[where] += rows_down(jnp.where(far, high, low), row_shift)
        return carried

    lax.fori_loop(0, live, visit, 0)
    copies = [
        pltpu.make_async_copy(totals.at[:, pl.ds(0, margin), :], up_ref, sems.at[0, 0]),
        pltpu.make_async_copy(
            totals.at[:, pl.ds(margin + tile_rows, margin), :], down_ref, sems.at[0, 1]
        ),
        pltpu.make_async_copy(update_ref, update_out, sems.at[0, 2]),
    ] + [
        pltpu.make_async_copy(
            totals.at[part, pl.ds(margin, tile_rows), :], middle_ref.at[part], sems.at[1, part]
        )
        for part in range(2)
    ]
    for copy in copies:
        copy.start()
    for copy in copies:
        copy.wait()


def gradients(offsets, counts, extended, probe, patterns, table):
    slots, width = patterns.shape[:2]
    modes = probe.shape[1]
    margin = width // 2
    full = extended.shape
    tile_rows = full[1] - 2 * margin
    anywhere = pl.BlockSpec(memory_space=pl.ANY)
    scalars = pl.BlockSpec(memory_space=pltpu.SMEM)
    flops = slots * modes * 8 * 2 * width**3
    return pl.pallas_call(
        kernel,
        in_specs=[scalars] * 2 + [anywhere] * 4,
        out_specs=[anywhere] * 4,
        scratch_shapes=[
            pltpu.VMEM((2, 2, width + SUB, width + LANES), F32),
            pltpu.VMEM((2, 2, width, width // 2), F32),
            pltpu.VMEM(probe.shape, BF16),
            pltpu.VMEM(table.shape, BF16),
            pltpu.VMEM(full, F32),
            pltpu.VMEM(probe.shape, F32),
            pltpu.VMEM((2, width, width), F32),
            pltpu.VMEM((modes, 2, width, width), BF16),
            pltpu.VMEM((modes, 2, width, width), F32),
            pltpu.VMEM((modes, 2, width, width), BF16),
            pltpu.VMEM((2, width // 2, width), F32),
            pltpu.VMEM((2, width, width), F32),
            pltpu.SemaphoreType.DMA((3, 3)),
        ],
        out_shape=[
            jax.ShapeDtypeStruct((2, margin, full[2]), F32),
            jax.ShapeDtypeStruct((2, tile_rows, full[2]), F32),
            jax.ShapeDtypeStruct((2, margin, full[2]), F32),
            jax.ShapeDtypeStruct(probe.shape, F32),
        ],
        compiler_params=pltpu.CompilerParams(vmem_limit_bytes=60 * 2**20),
        cost_estimate=pl.CostEstimate(
            flops=flops, bytes_accessed=16 * 2**20, transcendentals=slots * width * width
        ),
    )(offsets, counts, extended, probe, patterns, table)


class Move:
    def __init__(self, src, dst, sems, index, target, sends=None, lands=None):
        self.copy = pltpu.make_async_remote_copy(
            src_ref=src,
            dst_ref=dst,
            send_sem=sems[0].at[index],
            recv_sem=sems[1].at[index],
            device_id=target,
            device_id_type=pl.DeviceIdType.MESH,
        )
        self.sends = sends
        self.lands = lands

    def start(self):
        when(self.sends, self.copy.start)

    def arrive(self):
        when(self.lands, self.copy.wait_recv)

    def leave(self):
        when(self.sends, self.copy.wait_send)


def when(condition, action):
    if condition is None:
        action()
    else:
        pl.when(condition)(lambda: action())


class Place:
    def __init__(self):
        self.row, self.col = lax.axis_index("row"), lax.axis_index("col")
        self.rows, self.cols = lax.axis_size("row"), lax.axis_size("col")
        self.has_up, self.has_down = self.row > 0, self.row < self.rows - 1
        self.has_left, self.has_right = self.col > 0, self.col < self.cols - 1
        self.up, self.down = (self.row - 1, self.col), (self.row + 1, self.col)
        self.left, self.right = (self.row, self.col - 1), (self.row, self.col + 1)

    def greet(self, others=()):
        barrier = pltpu.get_barrier_semaphore()
        near = [
            (self.has_up, self.up),
            (self.has_down, self.down),
            (self.has_left, self.left),
            (self.has_right, self.right),
        ]

        def signal(target):
            pl.semaphore_signal(
                barrier, inc=1, device_id=target, device_id_type=pl.DeviceIdType.MESH
            )

        for condition, target in near:
            when(condition, lambda target=target: signal(target))
        for target in others:
            signal(target)
        peers = sum(condition.astype(jnp.int32) for condition, _ in near)
        pl.semaphore_wait(barrier, peers + len(others))


def halo_kernel(object_ref, out_ref, ext, send_sems, recv_sems, local_sems):
    me = Place()
    tile_rows, tile_cols = object_ref.shape[1:]
    margin = (out_ref.shape[1] - tile_rows) // 2
    sems = (send_sems, recv_sems)
    body, centre = pl.ds(margin, tile_rows), pl.ds(margin, tile_cols)
    first, beyond = pl.ds(0, margin), pl.ds(margin + tile_cols, margin)
    above, below = pl.ds(0, margin), pl.ds(margin + tile_rows, margin)
    left, right = pl.ds(margin, margin), pl.ds(tile_cols, margin)
    bands = [(margin, margin), (tile_rows, margin)]
    if tile_rows > 2 * margin:
        bands.append((2 * margin, tile_rows - 2 * margin))
    loads = [
        pltpu.make_async_copy(
            object_ref.at[:, pl.ds(start - margin, rows), :],
            ext.at[:, pl.ds(start, rows), centre],
            local_sems.at[number],
        )
        for number, (start, rows) in enumerate(bands)
    ]
    for load in loads:
        load.start()
    me.greet()
    count = iter(range(send_sems.shape[0]))

    sides = []
    strips = []
    for number, (start, rows) in enumerate(bands):
        band = pl.ds(start, rows)
        loads[number].wait()
        pair = (
            Move(ext.at[:, band, right], ext.at[:, band, first], sems, next(count),
                 me.right, me.has_right, me.has_left),
            Move(ext.at[:, band, left], ext.at[:, band, beyond], sems, next(count),
                 me.left, me.has_left, me.has_right),
        )
        sides.append(pair)
        if number == 0:
            strips.append(
                Move(ext.at[:, band, centre], ext.at[:, below, centre], sems, next(count),
                     me.up, me.has_up, me.has_down)
            )
        if number == 1:
            strips.append(
                Move(ext.at[:, band, centre], ext.at[:, above, centre], sems, next(count),
                     me.down, me.has_down, me.has_up)
            )
        for move in pair:
            move.start()
        if number < 2:
            strips[number].start()
    stores = [
        pltpu.make_async_copy(
            ext.at[:, body, centre], out_ref.at[:, body, centre], local_sems.at[3]
        )
    ]
    stores[0].start()
    corners = []
    for number, (target, sends, lands, rows) in enumerate(
        [(me.up, me.has_up, me.has_down, below), (me.down, me.has_down, me.has_up, above)]
    ):
        band = pl.ds(*bands[number])
        for side, (cols, has) in enumerate([(first, me.has_left), (beyond, me.has_right)]):
            sides[number][side].arrive()
            move = Move(ext.at[:, band, cols], ext.at[:, rows, cols], sems, next(count),
                        target, jnp.logical_and(sends, has), jnp.logical_and(lands, has))
            move.start()
            corners.append(move)
    for pair in sides[2:]:
        for move in pair:
            move.arrive()
    for number, cols in enumerate((first, beyond)):
        stores.append(
            pltpu.make_async_copy(
                ext.at[:, body, cols], out_ref.at[:, body, cols], local_sems.at[4 + number]
            )
        )
        stores[-1].start()
    for move in strips + corners:
        move.arrive()
    for number, rows in enumerate((above, below)):
        stores.append(
            pltpu.make_async_copy(
                ext.at[:, rows, :], out_ref.at[:, rows, :], local_sems.at[6 + number]
            )
        )
        stores[-1].start()
    for move in [move for pair in sides for move in pair] + strips + corners:
        move.leave()
    for store in stores:
        store.wait()


def halo(object_field, margin):
    tile_rows, tile_cols = object_field.shape[1:]
    anywhere = pl.BlockSpec(memory_space=pl.ANY)
    return pl.pallas_call(
        halo_kernel,
        in_specs=[anywhere],
        out_specs=anywhere,
        out_shape=jax.ShapeDtypeStruct((2, tile_rows + 2 * margin, tile_cols + 2 * margin), F32),
        scratch_shapes=[
            pltpu.VMEM((2, tile_rows + 2 * margin, tile_cols + 2 * margin), F32),
            pltpu.SemaphoreType.DMA((12,)),
            pltpu.SemaphoreType.DMA((12,)),
            pltpu.SemaphoreType.DMA((8,)),
        ],
        compiler_params=pltpu.CompilerParams(
            collective_id=0, has_side_effects=True, vmem_limit_bytes=60 * 2**20
        ),
    )(object_field)


def bits_of(count):
    return [1 << i for i in range(count.bit_length() - 1)]


def last_kernel(
    up_hbm, middle_ref, down_hbm, update_ref,
    object_ref, probe_ref,
    up_ref, down_ref, above, below, from_left, from_right, edges, total, landed,
    send_sems, recv_sems, sum_send, sum_recv, local_sems,
):
    me = Place()
    tile_rows, tile_cols = object_ref.shape[1:]
    margin = up_ref.shape[1]
    sems = (send_sems, recv_sems)
    head, tail = pl.ds(0, margin), pl.ds(tile_rows - margin, margin)
    first, beyond = pl.ds(0, margin), pl.ds(margin + tile_cols, margin)
    centre = pl.ds(margin, tile_cols)

    row_bits = [("row", bit) for bit in bits_of(me.rows)]
    col_bits = [("col", bit) for bit in bits_of(me.cols)]
    orders = [row_bits + col_bits, row_bits[:1] + row_bits[:0:-1] + col_bits]

    def partner(axis, bit):
        flip = lambda at: at + bit - 2 * bit * (at // bit % 2)
        return (flip(me.row), me.col) if axis == "row" else (me.row, flip(me.col))

    def half_of(axis, bit):
        return (me.row if axis == "row" else me.col) // bit % 2

    local = [
        pltpu.make_async_copy(update_ref, total, local_sems.at[0]),
        pltpu.make_async_copy(up_hbm, up_ref, local_sems.at[1]),
        pltpu.make_async_copy(down_hbm, down_ref, local_sems.at[2]),
        pltpu.make_async_copy(middle_ref.at[:, :, first], edges.at[0], local_sems.at[3]),
        pltpu.make_async_copy(middle_ref.at[:, :, beyond], edges.at[1], local_sems.at[4]),
        pltpu.make_async_copy(middle_ref.at[:, :, centre], object_ref, local_sems.at[5]),
    ]
    for copy in local:
        copy.start()
    me.greet([partner(axis, bit) for axis, bit in orders[0] if bit > 1])

    count = iter(range(send_sems.shape[0]))
    corners = []
    for cols in (first, beyond):
        corners.append(
            (
                Move(down_ref.at[:, :, cols], above.at[:, :, cols], sems, next(count),
                     me.down, me.has_down, me.has_up),
                Move(up_ref.at[:, :, cols], below.at[:, :, cols], sems, next(count),
                     me.up, me.has_up, me.has_down),
            )
        )

    size = update_ref.shape[0]
    bases = [[0], [0]]

    def halving(stream, step):
        lanes = pl.ds(stream * LANES, LANES)
        axis, bit = orders[stream][step]
        rows = size >> (step + 1)
        half = half_of(axis, bit)
        base = bases[stream][step]
        keep = pl.multiple_of(base + half * rows, SUB)
        give = pl.multiple_of(base + (1 - half) * rows, SUB)
        bases[stream].append(keep)
        return Move(
            total.at[pl.ds(give, rows), lanes],
            landed.at[pl.ds(size - 2 * rows, rows), lanes],
            (sum_send.at[stream], sum_recv.at[stream]), step, partner(axis, bit),
        )

    def add_half(stream, step, out_ref):
        lanes = pl.ds(stream * LANES, LANES)
        rows = size >> (step + 1)
        here = (pl.ds(bases[stream][step + 1], rows), lanes)
        out_ref[here] = total[here] + landed[pl.ds(size - 2 * rows, rows), lanes]

    def doubling(stream, step):
        lanes = pl.ds(stream * LANES, LANES)
        axis, bit = orders[stream][step]
        here = (pl.ds(bases[stream][step + 1], size >> (step + 1)), lanes)
        return Move(
            probe_ref.at[here], probe_ref.at[here],
            (sum_send.at[stream], sum_recv.at[stream]), steps + step, partner(axis, bit),
        )

    steps = len(orders[0])
    streams = range(2)
    sums = []
    current = [halving(stream, 0) for stream in streams]
    local[0].wait()
    for move in current:
        move.start()
    local[1].wait()
    local[2].wait()
    for pair in corners:
        for move in pair:
            move.start()
    local[3].wait()
    local[4].wait()

    flats = []
    if tile_rows > 2 * margin:
        inner = pl.ds(margin, tile_rows - 2 * margin)
        flats = [
            Move(edges.at[1, :, inner, :], from_left.at[:, inner, :], sems, next(count),
                 me.right, me.has_right, me.has_left),
            Move(edges.at[0, :, inner, :], from_right.at[:, inner, :], sems, next(count),
                 me.left, me.has_left, me.has_right),
        ]
    for move in flats:
        move.start()
    ends = []

    def send_ends():
        for side, (cols, out_ref, target, sends, lands) in enumerate(
            [
                (first, from_right, me.left, me.has_left, me.has_right),
                (beyond, from_left, me.right, me.has_right, me.has_left),
            ]
        ):
            for end, (band, got, has) in enumerate(
                [(head, above, me.has_up), (tail, below, me.has_down)]
            ):
                corners[side][end].arrive()

                def add(side=side, band=band, got=got, cols=cols):
                    edges[side, :, band, :] += got[:, :, cols]

                when(has, add)
                move = Move(edges.at[side, :, band, :], out_ref.at[:, band, :], sems, next(count),
                            target, sends, lands)
                move.start()
                ends.append(move)

    for step in range(steps):
        for stream in streams:
            move = current[stream]
            move.arrive()
            sums.append(move)
            add_half(stream, step, total if step < steps - 1 else probe_ref)
            if step < steps - 1:
                current[stream] = halving(stream, step + 1)
            else:
                current[stream] = doubling(stream, step)
            current[stream].start()
        if step == 0:
            send_ends()
        if step == len(row_bits) - 1:
            strips = [
                Move(down_ref.at[:, :, centre], above.at[:, :, centre], sems, next(count),
                     me.down, me.has_down, me.has_up),
                Move(up_ref.at[:, :, centre], below.at[:, :, centre], sems, next(count),
                     me.up, me.has_up, me.has_down),
            ]
            for move in strips:
                move.start()
            flats += strips
    for step in range(steps - 1, -1, -1):
        for stream in streams:
            move = current[stream]
            move.arrive()
            sums.append(move)
            if step > 0:
                current[stream] = doubling(stream, step - 1)
                current[stream].start()

    local[5].wait()
    for move in flats + ends:
        move.arrive()

    def from_above():
        object_ref[:, :margin, :] += above[:, :, margin : margin + tile_cols]

    def from_below():
        object_ref[:, tile_rows - margin :, :] += below[:, :, margin : margin + tile_cols]

    def add_left():
        object_ref[:, :, :margin] += from_left[...]

    def add_right():
        object_ref[:, :, tile_cols - margin :] += from_right[...]

    when(me.has_up, from_above)
    when(me.has_down, from_below)
    when(me.has_left, add_left)
    when(me.has_right, add_right)
    for move in [move for pair in corners for move in pair] + flats + ends + sums:
        move.leave()


def finish(up, middle, down, update):
    margin = up.shape[1]
    tile_rows = middle.shape[1]
    tile_cols = middle.shape[2] - 2 * margin
    width = update.shape[-1]
    flat = update.reshape(-1, width)
    steps = len(bits_of(lax.axis_size("row") * lax.axis_size("col")))
    vmem = pl.BlockSpec(memory_space=pltpu.VMEM)
    object_grad, probe_grad = pl.pallas_call(
        last_kernel,
        in_specs=[pl.BlockSpec(memory_space=pl.ANY)] * 4,
        out_specs=[vmem, vmem],
        out_shape=[
            jax.ShapeDtypeStruct((2, tile_rows, tile_cols), F32),
            jax.ShapeDtypeStruct(flat.shape, F32),
        ],
        scratch_shapes=[
            pltpu.VMEM(up.shape, F32),
            pltpu.VMEM(up.shape, F32),
            pltpu.VMEM(up.shape, F32),
            pltpu.VMEM(up.shape, F32),
            pltpu.VMEM((2, tile_rows, margin), F32),
            pltpu.VMEM((2, tile_rows, margin), F32),
            pltpu.VMEM((2, 2, tile_rows, margin), F32),
            pltpu.VMEM(flat.shape, F32),
            pltpu.VMEM(flat.shape, F32),
            pltpu.SemaphoreType.DMA((12,)),
            pltpu.SemaphoreType.DMA((12,)),
            pltpu.SemaphoreType.DMA((2, 2 * steps)),
            pltpu.SemaphoreType.DMA((2, 2 * steps)),
            pltpu.SemaphoreType.DMA((6,)),
        ],
        compiler_params=pltpu.CompilerParams(
            collective_id=1, has_side_effects=True, vmem_limit_bytes=60 * 2**20
        ),
    )(up, middle, down, flat)
    return object_grad, probe_grad.reshape(update.shape)


def on_device(object_field, probe, patterns, offsets, counts):
    width = patterns.shape[1]
    table = jnp.asarray(tables(width))
    extended = halo(object_field, width // 2)
    up, middle, down, update = gradients(offsets, counts, extended, probe, patterns, table)
    return finish(up, middle, down, update)


def solution(mesh):
    in_specs = (
        P(None, "row", "col"),
        P(),
        P(("row", "col"), None, None),
        P(None, ("row", "col")),
        P("row", "col"),
    )
    out_specs = (P(None, "row", "col"), P())
    return jax.shard_map(
        on_device, mesh=mesh, in_specs=in_specs, out_specs=out_specs, check_vma=False
    )
```

```python
import math

import jax
import jax.numpy as jnp
import ml_dtypes
import numpy as np
from jax import lax
from jax.experimental import pallas as pl
from jax.experimental.pallas import tpu as pltpu
from jax.sharding import PartitionSpec as P

F32 = jnp.float32
BF16 = jnp.bfloat16


def tables(length):
    index = np.arange(length)
    product = index[:, None] * index[None, :] % length
    angle = product.astype(np.float32) * np.float32(2.0 * math.pi / length)
    factor = np.float32(1.0 / math.sqrt(length))
    re = (np.cos(angle) * factor).astype(ml_dtypes.bfloat16)
    im = (-np.sin(angle) * factor).astype(ml_dtypes.bfloat16)
    half = length // 2
    right = []
    left = []
    for parity in range(2):
        a, b = re[:half, parity::2], im[:half, parity::2]
        right.append(np.block([[a, b], [-b, a]]))
        a, b = re[parity::2, :half], im[parity::2, :half]
        left.append(np.block([[a, -b], [b, a]]))
    order = np.concatenate([index[0::2], index[1::2]])
    spread = (index[:, None] == order[None, :]).astype(ml_dtypes.bfloat16)
    return np.stack(right + left + [spread])


def mm(a, b):
    return jnp.dot(a, b, preferred_element_type=F32)


SUB = 8
LANES = 128


def rows_up(block, shift):
    tiles = block.reshape(-1, SUB, LANES)
    tiles = pltpu.roll(tiles, lax.rem(SUB - shift, SUB), 1)
    near = lax.broadcasted_iota(jnp.int32, (1, SUB, LANES), 1) < SUB - shift
    return jnp.where(near, tiles[:-1], tiles[1:]).reshape(-1, LANES)


def rows_down(block, shift):
    tiles = pltpu.roll(block.reshape(-1, SUB, LANES), lax.rem(shift, SUB), 1)
    near = lax.broadcasted_iota(jnp.int32, (1, SUB, LANES), 1) >= shift
    zero = jnp.zeros((1, SUB, LANES), F32)
    high = jnp.concatenate([tiles, zero], axis=0)
    low = jnp.concatenate([zero, tiles], axis=0)
    return jnp.where(near, high, low).reshape(-1, LANES)


def kernel(
    offsets_ref, count_ref,
    extended_ref, probe_hbm, patterns_ref, table_hbm,
    up_ref, middle_ref, down_ref, update_out,
    window, pattern, probe_ref, table_ref, totals, update_ref, patch, mixed, field, residual,
    wide_ref, measured_ref, term, sems,
):
    margin, tile_rows = up_ref.shape[1], middle_ref.shape[1]
    modes, width = probe_ref.shape[1:3]
    tile_cols = middle_ref.shape[2] - 2 * margin
    half = width // 2
    lanes = LANES
    tall, wide = window.shape[2:]
    chunk = 16
    live = count_ref[0, 0]
    first_row = lax.axis_index("row") * tile_rows - margin
    first_col = lax.axis_index("col") * tile_cols - margin

    def corner(number):
        row = offsets_ref[0, number] - first_row
        col = offsets_ref[1, number] - first_col
        row_base = jnp.minimum(row // SUB * SUB, totals.shape[1] - tall)
        col_base = jnp.minimum(col // lanes * lanes, totals.shape[2] - wide)
        return (
            pl.multiple_of(row_base, SUB), row - row_base,
            pl.multiple_of(col_base, lanes), col - col_base,
        )

    def fetches(number):
        slot = lax.rem(number, 2)
        row_base, _, col_base, _ = corner(number)
        return [
            pltpu.make_async_copy(
                extended_ref.at[:, pl.ds(row_base, tall), pl.ds(col_base, wide)],
                window.at[slot], sems.at[slot, 0],
            )
        ] + [
            pltpu.make_async_copy(
                patterns_ref.at[number, :, pl.ds(side * half, half)],
                pattern.at[slot, side], sems.at[slot, 1 + side],
            )
            for side in range(2)
        ]

    constants = [
        pltpu.make_async_copy(table_hbm, table_ref, sems.at[2, 0]),
        pltpu.make_async_copy(probe_hbm, probe_ref, sems.at[2, 1]),
    ]
    for copy in fetches(0) + constants:
        copy.start()
    totals[...] = jnp.zeros_like(totals)
    update_ref[...] = jnp.zeros_like(update_ref)
    for copy in constants:
        copy.wait()

    def visit(number, carried):
        slot = lax.rem(number, 2)
        row_base, row_shift, base, shift = corner(number)

        @pl.when(number + 1 < live)
        def _():
            for copy in fetches(number + 1):
                copy.start()

        for copy in fetches(number):
            copy.wait()

        lane = lax.broadcasted_iota(jnp.int32, (width, lanes), 1)
        back = lax.rem(lanes - shift, lanes)
        ahead = lax.rem(shift, lanes)
        near = lane < lanes - shift
        for part in range(2):
            pieces = [
                pltpu.roll(
                    rows_up(window[slot, part, :, t * lanes : (t + 1) * lanes], row_shift), back, 1
                )
                for t in range(width // lanes + 1)
            ]
            for t in range(width // lanes):
                patch[part, :, t * lanes : (t + 1) * lanes] = jnp.where(
                    near, pieces[t], pieces[t + 1]
                )

        r_even, r_odd = table_ref[0], table_ref[1]
        l_even, l_odd = table_ref[2], table_ref[3]
        spread = table_ref[4]

        fine = []
        for parity in range(2):
            rows_of = pl.ds(parity, half, 2)
            measured = jnp.concatenate(
                [pattern[slot, 0, rows_of, :], pattern[slot, 1, rows_of, :]], axis=1
            )
            fine.append(measured.astype(BF16))
            fine.append((measured - fine[-1].astype(F32)).astype(BF16))
        parts = mm(jnp.concatenate(fine, axis=0), spread)
        for parity in range(2):
            start = parity * width
            measured_ref[parity] = parts[start : start + half] + parts[start + half : start + width]

        for k in range(modes):
            for start in range(0, width, chunk):
                here = slice(start, start + chunk)
                there = slice(k * width + start, k * width + start + chunk)
                o_re, o_im = patch[0, here], patch[1, here]
                p_re = probe_ref[0, k, here].astype(F32)
                p_im = probe_ref[1, k, here].astype(F32)
                x_re = p_re * o_re - p_im * o_im
                x_im = p_re * o_im + p_im * o_re
                mixed[0, there, :half] = (x_re[:, :half] + x_re[:, half:]).astype(BF16)
                mixed[0, there, half:] = (x_im[:, :half] + x_im[:, half:]).astype(BF16)
                mixed[1, there, :half] = (x_re[:, :half] - x_re[:, half:]).astype(BF16)
                mixed[1, there, half:] = (x_im[:, :half] - x_im[:, half:]).astype(BF16)
        wide_ref[0] = mm(mixed[0], r_even)
        wide_ref[1] = mm(mixed[1], r_odd)
        for k in range(modes):
            there = slice(k * width, (k + 1) * width)
            y_even, y_odd = wide_ref[0, there], wide_ref[1, there]
            for parity, table in enumerate((l_even, l_odd)):
                if parity == 0:
                    a = y_even[:half] + y_even[half:]
                    b = y_odd[:half] + y_odd[half:]
                else:
                    a = y_even[:half] - y_even[half:]
                    b = y_odd[:half] - y_odd[half:]
                u = jnp.concatenate(
                    [
                        jnp.concatenate([a[:, :half], b[:, :half]], axis=1),
                        jnp.concatenate([a[:, half:], b[:, half:]], axis=1),
                    ],
                    axis=0,
                ).astype(BF16)
                field[k, parity] = mm(table, u)

        for parity in range(2):
            for start in range(0, half, chunk):
                top = slice(start, start + chunk)
                low = slice(half + start, half + start + chunk)
                here = slice(parity * half + start, parity * half + start + chunk)
                waves = [(field[k, parity, top], field[k, parity, low]) for k in range(modes)]
                intensity = sum(re * re + im * im for re, im in waves)
                ratio = 1.0 - measured_ref[parity, top] * lax.rsqrt(jnp.maximum(intensity, 1.0))
                for k, (re, im) in enumerate(waves):
                    c_re = (re * ratio).astype(BF16)
                    c_im = (im * ratio).astype(BF16)
                    there = slice(k * width + here.start, k * width + here.stop)
                    residual[0, there, :half] = c_re[:, :half]
                    residual[0, there, half:] = c_im[:, :half]
                    residual[1, there, :half] = c_re[:, half:]
                    residual[1, there, half:] = c_im[:, half:]

        wide_ref[0] = mm(residual[0], l_even)
        wide_ref[1] = mm(residual[1], l_odd)
        for k in range(modes):
            there = slice(k * width, (k + 1) * width)
            g_even, g_odd = wide_ref[0, there], wide_ref[1, there]
            a = g_even + g_odd
            b = g_even - g_odd
            for parity, table in enumerate((r_even, r_odd)):
                here = slice(parity * half, (parity + 1) * half)
                v = jnp.concatenate(
                    [
                        jnp.concatenate([a[here, :half], b[here, :half]], axis=1),
                        jnp.concatenate([a[here, half:], b[here, half:]], axis=1),
                    ],
                    axis=0,
                ).astype(BF16)
                field[k, parity] = mm(table, v)

        for start in range(0, half, chunk):
            for t in range(width // lanes):
                cols = slice(t * lanes, (t + 1) * lanes)
                top = (slice(start, start + chunk), cols)
                low = (slice(half + start, half + start + chunk), cols)
                terms = [[0.0, 0.0], [0.0, 0.0]]
                objects = [(patch[0, *here], patch[1, *here]) for here in (top, low)]
                for k in range(modes):
                    e_re, e_im = field[k, 0, *top], field[k, 0, *low]
                    d_re, d_im = field[k, 1, *top], field[k, 1, *low]
                    waves = [(e_re + d_re, e_im + d_im), (e_re - d_re, e_im - d_im)]
                    for part, here in enumerate((top, low)):
                        w_re, w_im = waves[part]
                        o_re, o_im = objects[part]
                        p_re = probe_ref[0, k, *here].astype(F32)
                        p_im = probe_ref[1, k, *here].astype(F32)
                        terms[part][0] += p_re * w_re + p_im * w_im
                        terms[part][1] += p_re * w_im - p_im * w_re
                        update_ref[0, k, *here] += o_re * w_re + o_im * w_im
                        update_ref[1, k, *here] += o_re * w_im - o_im * w_re
                for part, here in enumerate((top, low)):
                    term[0, *here] = terms[part][0]
                    term[1, *here] = terms[part][1]

        far = lane >= shift
        for part in range(2):
            pieces = [
                pltpu.roll(term[part, :, t * lanes : (t + 1) * lanes], ahead, 1)
                for t in range(width // lanes)
            ]
            for t in range(width // lanes + 1):
                low = pieces[t - 1] if t > 0 else 0.0
                high = pieces[t] if t < width // lanes else 0.0
                where = (part, pl.ds(row_base, tall), pl.ds(base + t * lanes, lanes))
                totals[where] += rows_down(jnp.where(far, high, low), row_shift)
        return carried

    lax.fori_loop(0, live, visit, 0)
    copies = [
        pltpu.make_async_copy(totals.at[:, pl.ds(0, margin), :], up_ref, sems.at[0, 0]),
        pltpu.make_async_copy(
            totals.at[:, pl.ds(margin + tile_rows, margin), :], down_ref, sems.at[0, 1]
        ),
        pltpu.make_async_copy(update_ref, update_out, sems.at[0, 2]),
    ] + [
        pltpu.make_async_copy(
            totals.at[part, pl.ds(margin, tile_rows), :], middle_ref.at[part], sems.at[1, part]
        )
        for part in range(2)
    ]
    for copy in copies:
        copy.start()
    for copy in copies:
        copy.wait()


def gradients(offsets, counts, extended, probe, patterns, table):
    slots, width = patterns.shape[:2]
    modes = probe.shape[1]
    margin = width // 2
    full = extended.shape
    tile_rows = full[1] - 2 * margin
    anywhere = pl.BlockSpec(memory_space=pl.ANY)
    scalars = pl.BlockSpec(memory_space=pltpu.SMEM)
    flops = slots * modes * 8 * 2 * width**3
    return pl.pallas_call(
        kernel,
        in_specs=[scalars] * 2 + [anywhere] * 4,
        out_specs=[anywhere] * 4,
        scratch_shapes=[
            pltpu.VMEM((2, 2, width + SUB, width + LANES), F32),
            pltpu.VMEM((2, 2, width, width // 2), F32),
            pltpu.VMEM(probe.shape, BF16),
            pltpu.VMEM(table.shape, BF16),
            pltpu.VMEM(full, F32),
            pltpu.VMEM(probe.shape, F32),
            pltpu.VMEM((2, width, width), F32),
            pltpu.VMEM((2, modes * width, width), BF16),
            pltpu.VMEM((modes, 2, width, width), F32),
            pltpu.VMEM((2, modes * width, width), BF16),
            pltpu.VMEM((2, modes * width, width), F32),
            pltpu.VMEM((2, width // 2, width), F32),
            pltpu.VMEM((2, width, width), F32),
            pltpu.SemaphoreType.DMA((3, 3)),
        ],
        out_shape=[
            jax.ShapeDtypeStruct((2, margin, full[2]), F32),
            jax.ShapeDtypeStruct((2, tile_rows, full[2]), F32),
            jax.ShapeDtypeStruct((2, margin, full[2]), F32),
            jax.ShapeDtypeStruct(probe.shape, F32),
        ],
        compiler_params=pltpu.CompilerParams(vmem_limit_bytes=60 * 2**20),
        cost_estimate=pl.CostEstimate(
            flops=flops, bytes_accessed=16 * 2**20, transcendentals=slots * width * width
        ),
    )(offsets, counts, extended, probe, patterns, table)


class Move:
    def __init__(self, src, dst, sems, index, target, sends=None, lands=None):
        self.copy = pltpu.make_async_remote_copy(
            src_ref=src,
            dst_ref=dst,
            send_sem=sems[0].at[index],
            recv_sem=sems[1].at[index],
            device_id=target,
            device_id_type=pl.DeviceIdType.MESH,
        )
        self.sends = sends
        self.lands = lands

    def start(self):
        when(self.sends, self.copy.start)

    def arrive(self):
        when(self.lands, self.copy.wait_recv)

    def leave(self):
        when(self.sends, self.copy.wait_send)


def when(condition, action):
    if condition is None:
        action()
    else:
        pl.when(condition)(lambda: action())


class Place:
    def __init__(self):
        self.row, self.col = lax.axis_index("row"), lax.axis_index("col")
        self.rows, self.cols = lax.axis_size("row"), lax.axis_size("col")
        self.has_up, self.has_down = self.row > 0, self.row < self.rows - 1
        self.has_left, self.has_right = self.col > 0, self.col < self.cols - 1
        self.up, self.down = (self.row - 1, self.col), (self.row + 1, self.col)
        self.left, self.right = (self.row, self.col - 1), (self.row, self.col + 1)

    def greet(self, others=()):
        barrier = pltpu.get_barrier_semaphore()
        near = [
            (self.has_up, self.up),
            (self.has_down, self.down),
            (self.has_left, self.left),
            (self.has_right, self.right),
        ]

        def signal(target):
            pl.semaphore_signal(
                barrier, inc=1, device_id=target, device_id_type=pl.DeviceIdType.MESH
            )

        for condition, target in near:
            when(condition, lambda target=target: signal(target))
        for target in others:
            signal(target)
        peers = sum(condition.astype(jnp.int32) for condition, _ in near)
        pl.semaphore_wait(barrier, peers + len(others))


def halo_kernel(object_ref, out_ref, ext, send_sems, recv_sems, local_sems):
    me = Place()
    tile_rows, tile_cols = object_ref.shape[1:]
    margin = (out_ref.shape[1] - tile_rows) // 2
    sems = (send_sems, recv_sems)
    body, centre = pl.ds(margin, tile_rows), pl.ds(margin, tile_cols)
    first, beyond = pl.ds(0, margin), pl.ds(margin + tile_cols, margin)
    above, below = pl.ds(0, margin), pl.ds(margin + tile_rows, margin)
    left, right = pl.ds(margin, margin), pl.ds(tile_cols, margin)
    bands = [(margin, margin), (tile_rows, margin)]
    if tile_rows > 2 * margin:
        bands.append((2 * margin, tile_rows - 2 * margin))
    loads = [
        pltpu.make_async_copy(
            object_ref.at[:, pl.ds(start - margin, rows), :],
            ext.at[:, pl.ds(start, rows), centre],
            local_sems.at[number],
        )
        for number, (start, rows) in enumerate(bands)
    ]
    for load in loads:
        load.start()
    me.greet()
    count = iter(range(send_sems.shape[0]))

    sides = []
    strips = []
    for number, (start, rows) in enumerate(bands):
        band = pl.ds(start, rows)
        loads[number].wait()
        pair = (
            Move(ext.at[:, band, right], ext.at[:, band, first], sems, next(count),
                 me.right, me.has_right, me.has_left),
            Move(ext.at[:, band, left], ext.at[:, band, beyond], sems, next(count),
                 me.left, me.has_left, me.has_right),
        )
        sides.append(pair)
        if number == 0:
            strips.append(
                Move(ext.at[:, band, centre], ext.at[:, below, centre], sems, next(count),
                     me.up, me.has_up, me.has_down)
            )
        if number == 1:
            strips.append(
                Move(ext.at[:, band, centre], ext.at[:, above, centre], sems, next(count),
                     me.down, me.has_down, me.has_up)
            )
        for move in pair:
            move.start()
        if number < 2:
            strips[number].start()
    stores = [
        pltpu.make_async_copy(
            ext.at[:, body, centre], out_ref.at[:, body, centre], local_sems.at[3]
        )
    ]
    stores[0].start()
    corners = []
    for number, (target, sends, lands, rows) in enumerate(
        [(me.up, me.has_up, me.has_down, below), (me.down, me.has_down, me.has_up, above)]
    ):
        band = pl.ds(*bands[number])
        for side, (cols, has) in enumerate([(first, me.has_left), (beyond, me.has_right)]):
            sides[number][side].arrive()
            move = Move(ext.at[:, band, cols], ext.at[:, rows, cols], sems, next(count),
                        target, jnp.logical_and(sends, has), jnp.logical_and(lands, has))
            move.start()
            corners.append(move)
    for pair in sides[2:]:
        for move in pair:
            move.arrive()
    for number, cols in enumerate((first, beyond)):
        stores.append(
            pltpu.make_async_copy(
                ext.at[:, body, cols], out_ref.at[:, body, cols], local_sems.at[4 + number]
            )
        )
        stores[-1].start()
    for move in strips + corners:
        move.arrive()
    for number, rows in enumerate((above, below)):
        stores.append(
            pltpu.make_async_copy(
                ext.at[:, rows, :], out_ref.at[:, rows, :], local_sems.at[6 + number]
            )
        )
        stores[-1].start()
    for move in [move for pair in sides for move in pair] + strips + corners:
        move.leave()
    for store in stores:
        store.wait()


def halo(object_field, margin):
    tile_rows, tile_cols = object_field.shape[1:]
    anywhere = pl.BlockSpec(memory_space=pl.ANY)
    return pl.pallas_call(
        halo_kernel,
        in_specs=[anywhere],
        out_specs=anywhere,
        out_shape=jax.ShapeDtypeStruct((2, tile_rows + 2 * margin, tile_cols + 2 * margin), F32),
        scratch_shapes=[
            pltpu.VMEM((2, tile_rows + 2 * margin, tile_cols + 2 * margin), F32),
            pltpu.SemaphoreType.DMA((12,)),
            pltpu.SemaphoreType.DMA((12,)),
            pltpu.SemaphoreType.DMA((8,)),
        ],
        compiler_params=pltpu.CompilerParams(
            collective_id=0, has_side_effects=True, vmem_limit_bytes=60 * 2**20
        ),
    )(object_field)


def bits_of(count):
    return [1 << i for i in range(count.bit_length() - 1)]


def last_kernel(
    up_hbm, middle_ref, down_hbm, update_ref,
    object_ref, probe_ref,
    up_ref, down_ref, above, below, from_left, from_right, edges, total, landed,
    send_sems, recv_sems, sum_send, sum_recv, local_sems,
):
    me = Place()
    tile_rows, tile_cols = object_ref.shape[1:]
    margin = up_ref.shape[1]
    sems = (send_sems, recv_sems)
    head, tail = pl.ds(0, margin), pl.ds(tile_rows - margin, margin)
    first, beyond = pl.ds(0, margin), pl.ds(margin + tile_cols, margin)
    centre = pl.ds(margin, tile_cols)

    row_bits = [("row", bit) for bit in bits_of(me.rows)]
    col_bits = [("col", bit) for bit in bits_of(me.cols)]
    orders = [
        row_bits + col_bits,
        row_bits[:1] + row_bits[:0:-1] + col_bits,
        row_bits[:1] + col_bits + row_bits[1:],
    ]

    def partner(axis, bit):
        flip = lambda at: at + bit - 2 * bit * (at // bit % 2)
        return (flip(me.row), me.col) if axis == "row" else (me.row, flip(me.col))

    def half_of(axis, bit):
        return (me.row if axis == "row" else me.col) // bit % 2

    local = [
        pltpu.make_async_copy(update_ref, total, local_sems.at[0]),
        pltpu.make_async_copy(up_hbm, up_ref, local_sems.at[1]),
        pltpu.make_async_copy(down_hbm, down_ref, local_sems.at[2]),
        pltpu.make_async_copy(middle_ref.at[:, :, first], edges.at[0], local_sems.at[3]),
        pltpu.make_async_copy(middle_ref.at[:, :, beyond], edges.at[1], local_sems.at[4]),
        pltpu.make_async_copy(middle_ref.at[:, :, centre], object_ref, local_sems.at[5]),
    ]
    for copy in local:
        copy.start()
    me.greet([partner(axis, bit) for axis, bit in orders[0] if bit > 1])

    count = iter(range(send_sems.shape[0]))
    corners = []
    for cols in (first, beyond):
        corners.append(
            (
                Move(down_ref.at[:, :, cols], above.at[:, :, cols], sems, next(count),
                     me.down, me.has_down, me.has_up),
                Move(up_ref.at[:, :, cols], below.at[:, :, cols], sems, next(count),
                     me.up, me.has_up, me.has_down),
            )
        )

    steps = len(orders[0])
    unit = SUB << steps
    units = update_ref.shape[0] // unit
    share = (3 * units + 4) // 8
    sizes = [share * unit, share * unit, (units - 2 * share) * unit]
    origins = [0, sizes[0], sizes[0] + sizes[1]]
    bases = [[origin] for origin in origins]
    streams = [stream for stream in range(3) if sizes[stream] > 0]

    def halving(stream, step):
        axis, bit = orders[stream][step]
        rows = sizes[stream] >> (step + 1)
        half = half_of(axis, bit)
        base = bases[stream][step]
        keep = pl.multiple_of(base + half * rows, SUB)
        give = pl.multiple_of(base + (1 - half) * rows, SUB)
        bases[stream].append(keep)
        return Move(
            total.at[pl.ds(give, rows)],
            landed.at[pl.ds(origins[stream] + sizes[stream] - 2 * rows, rows)],
            (sum_send.at[stream], sum_recv.at[stream]), step, partner(axis, bit),
        )

    def add_half(stream, step, out_ref):
        rows = sizes[stream] >> (step + 1)
        here = pl.ds(bases[stream][step + 1], rows)
        out_ref[here] = (
            total[here] + landed[pl.ds(origins[stream] + sizes[stream] - 2 * rows, rows)]
        )

    def doubling(stream, step):
        axis, bit = orders[stream][step]
        here = pl.ds(bases[stream][step + 1], sizes[stream] >> (step + 1))
        return Move(
            probe_ref.at[here], probe_ref.at[here],
            (sum_send.at[stream], sum_recv.at[stream]), steps + step, partner(axis, bit),
        )

    sums = []
    current = {stream: halving(stream, 0) for stream in streams}
    local[0].wait()
    for stream in streams:
        current[stream].start()
    local[1].wait()
    local[2].wait()
    for pair in corners:
        for move in pair:
            move.start()
    local[3].wait()
    local[4].wait()

    flats = []
    if tile_rows > 2 * margin:
        inner = pl.ds(margin, tile_rows - 2 * margin)
        flats = [
            Move(edges.at[1, :, inner, :], from_left.at[:, inner, :], sems, next(count),
                 me.right, me.has_right, me.has_left),
            Move(edges.at[0, :, inner, :], from_right.at[:, inner, :], sems, next(count),
                 me.left, me.has_left, me.has_right),
        ]
    for move in flats:
        move.start()
    ends = []

    def send_ends():
        for side, (cols, out_ref, target, sends, lands) in enumerate(
            [
                (first, from_right, me.left, me.has_left, me.has_right),
                (beyond, from_left, me.right, me.has_right, me.has_left),
            ]
        ):
            for end, (band, got, has) in enumerate(
                [(head, above, me.has_up), (tail, below, me.has_down)]
            ):
                corners[side][end].arrive()

                def add(side=side, band=band, got=got, cols=cols):
                    edges[side, :, band, :] += got[:, :, cols]

                when(has, add)
                move = Move(edges.at[side, :, band, :], out_ref.at[:, band, :], sems, next(count),
                            target, sends, lands)
                move.start()
                ends.append(move)

    for step in range(steps):
        for stream in streams:
            move = current[stream]
            move.arrive()
            sums.append(move)
            add_half(stream, step, total if step < steps - 1 else probe_ref)
            if step < steps - 1:
                current[stream] = halving(stream, step + 1)
            else:
                current[stream] = doubling(stream, step)
            current[stream].start()
        if step == 0:
            send_ends()
        if step == len(row_bits) - 1:
            strips = [
                Move(down_ref.at[:, :, centre], above.at[:, :, centre], sems, next(count),
                     me.down, me.has_down, me.has_up),
                Move(up_ref.at[:, :, centre], below.at[:, :, centre], sems, next(count),
                     me.up, me.has_up, me.has_down),
            ]
            for move in strips:
                move.start()
            flats += strips
    for step in range(steps - 1, -1, -1):
        for stream in streams:
            move = current[stream]
            move.arrive()
            sums.append(move)
            if step > 0:
                current[stream] = doubling(stream, step - 1)
                current[stream].start()

    local[5].wait()
    for move in flats + ends:
        move.arrive()

    def from_above():
        object_ref[:, :margin, :] += above[:, :, margin : margin + tile_cols]

    def from_below():
        object_ref[:, tile_rows - margin :, :] += below[:, :, margin : margin + tile_cols]

    def add_left():
        object_ref[:, :, :margin] += from_left[...]

    def add_right():
        object_ref[:, :, tile_cols - margin :] += from_right[...]

    when(me.has_up, from_above)
    when(me.has_down, from_below)
    when(me.has_left, add_left)
    when(me.has_right, add_right)
    for move in [move for pair in corners for move in pair] + flats + ends + sums:
        move.leave()


def finish(up, middle, down, update):
    margin = up.shape[1]
    tile_rows = middle.shape[1]
    tile_cols = middle.shape[2] - 2 * margin
    width = update.shape[-1]
    flat = update.reshape(-1, width)
    steps = len(bits_of(lax.axis_size("row") * lax.axis_size("col")))
    vmem = pl.BlockSpec(memory_space=pltpu.VMEM)
    object_grad, probe_grad = pl.pallas_call(
        last_kernel,
        in_specs=[pl.BlockSpec(memory_space=pl.ANY)] * 4,
        out_specs=[vmem, vmem],
        out_shape=[
            jax.ShapeDtypeStruct((2, tile_rows, tile_cols), F32),
            jax.ShapeDtypeStruct(flat.shape, F32),
        ],
        scratch_shapes=[
            pltpu.VMEM(up.shape, F32),
            pltpu.VMEM(up.shape, F32),
            pltpu.VMEM(up.shape, F32),
            pltpu.VMEM(up.shape, F32),
            pltpu.VMEM((2, tile_rows, margin), F32),
            pltpu.VMEM((2, tile_rows, margin), F32),
            pltpu.VMEM((2, 2, tile_rows, margin), F32),
            pltpu.VMEM(flat.shape, F32),
            pltpu.VMEM(flat.shape, F32),
            pltpu.SemaphoreType.DMA((12,)),
            pltpu.SemaphoreType.DMA((12,)),
            pltpu.SemaphoreType.DMA((3, 2 * steps)),
            pltpu.SemaphoreType.DMA((3, 2 * steps)),
            pltpu.SemaphoreType.DMA((6,)),
        ],
        compiler_params=pltpu.CompilerParams(
            collective_id=1, has_side_effects=True, vmem_limit_bytes=58 * 2**20
        ),
    )(up, middle, down, flat)
    return object_grad, probe_grad.reshape(update.shape)


def on_device(object_field, probe, patterns, offsets, counts):
    width = patterns.shape[1]
    table = jnp.asarray(tables(width))
    extended = halo(object_field, width // 2)
    up, middle, down, update = gradients(offsets, counts, extended, probe, patterns, table)
    return finish(up, middle, down, update)


def solution(mesh):
    in_specs = (
        P(None, "row", "col"),
        P(),
        P(("row", "col"), None, None),
        P(None, ("row", "col")),
        P("row", "col"),
    )
    out_specs = (P(None, "row", "col"), P())
    return jax.shard_map(
        on_device, mesh=mesh, in_specs=in_specs, out_specs=out_specs, check_vma=False
    )
```
